128 devices in a mesh: ctx: 16 (over y, z), kvh: 8 (over x, core).
Axes of the slice: x: 4, y: 4, z: 4, core: 2. Of those that a mesh axis runs over, the one named last changes fastest.
Arguments:
- queries: bfloat16 [8192, 4096], P('ctx', 'kvh'), may hold values from -113 to 113
- keys: bfloat16 [8192, 1024], P('ctx', 'kvh'), may hold values from -4.5 to 4.5
- values: bfloat16 [8192, 1024], P('ctx', 'kvh'), may hold values from -5 to 5
- span_order: int32 [16], replicated, may hold values from 0 to 15, each once
- ffn_input: bfloat16 [8192, 4096], P('ctx', 'kvh'), may hold values from -6 to 6
- norm_gain: float32 [4096], replicated, may hold values from 0.1 to 1.9
- gate_weight: bfloat16 [4096, 7168], P('ctx', 'kvh'), may hold values from -0.09375 to 0.09375
- up_weight: bfloat16 [4096, 7168], P('ctx', 'kvh'), may hold values from -0.09375 to 0.09375
- down_weight: bfloat16 [7168, 4096], P('kvh', 'ctx'), may hold values from -0.0625 to 0.0625
Outputs:
- attention: bfloat16 [8192, 4096], P('ctx', 'kvh')
- log_sums: float32 [32, 8192], P('kvh', 'ctx')
- ffn_out: bfloat16 [8192, 4096], P('ctx', 'kvh')
The draws below stay inside these ranges and needn't reach their ends.
Inputs may be any that keep to these rules, and one draw needn't show every extreme that they name: `span_order`: each span number appears once.
All inputs are finite; a program needn't handle non-finite values.
Results may differ from the reference program's by a relative error of at most 0.019.
Values may be sent and summed in bfloat16 or wider, within the bound.
A program may use at most 192 MiB of HBM per device.

```python
import math
import jax
import jax.numpy as jnp
from jax import lax

D = 4096
FF = 7168
H = 32
KVH = 8
HD = 128
TOK_DEV = 512
GROUP = 4
TOKENS = 8192
N_CTX = 16


def shared_keys(key):
    return jnp.clip(jax.random.normal(key, (N_CTX, TOK_DEV, KVH, HD), jnp.float32), -4.5, 4.5)


def draw_keys(key, part):
    base = shared_keys(key)
    return base.reshape(TOKENS, KVH * HD).astype(jnp.bfloat16)


def draw_queries(key, part):
    key = jax.random.fold_in(key, 11)
    fresh = jnp.clip(jax.random.normal(key, (N_CTX, TOK_DEV, KVH, GROUP, HD), jnp.float32), -4.5, 4.5)
    return fresh.reshape(TOKENS, H * HD).astype(jnp.bfloat16)


def block_scale(rng, shape, pieces, smallest, top_value):
    def one(axis_at, blocks):
        heights = jax.random.uniform(jax.random.fold_in(jax.random.fold_in(rng, 6), axis_at), (blocks,), jnp.float32, smallest / len(pieces), top_value / len(pieces))
        return jnp.repeat(jnp.exp(heights), shape[axis_at] // blocks).reshape((-1,) + (1,) * (len(shape) - axis_at - 1))

    loudness = one(*pieces[0])
    for cut in pieces[1:]:
        loudness = loudness * one(*cut)
    return loudness


def scatter_about(rng, extent, spread, reach, split=(), kind=jnp.bfloat16):
    result = jax.random.normal(rng, extent, jnp.float32) * spread
    if len(split) > 0:
        result = block_scale(rng, extent, split, -0.22, 0.18) * result
    return jnp.clip(result, min=-reach, max=reach).astype(kind)


def setup_inputs(seed: int = 0) -> dict:
    splits = jax.random.split(jax.random.key(seed), 10)
    queries = draw_queries(jax.random.fold_in(splits[9], 71), 0)
    keys = draw_keys(jax.random.fold_in(splits[9], 71), 0)
    values = scatter_about(splits[2], (TOKENS, KVH * HD), 1.0, 5.0, ((0, 16), (1, 8)))
    span_order = jax.random.permutation(splits[3], N_CTX).astype(jnp.int32)
    ffn_input = scatter_about(splits[4], (TOKENS, D), 1.0, 6.0, ((0, 16), (1, 8)))
    norm_gain = jnp.clip(1.0 + 0.18 * jax.random.normal(splits[5], (D,), jnp.float32), 0.1, 1.9)
    gate_weight = scatter_about(splits[6], (D, FF), D ** -0.5, 0.09375, ((0, 16), (1, 8)))
    up_weight = scatter_about(splits[7], (D, FF), D ** -0.5, 0.09375, ((0, 16), (1, 8)))
    down_weight = scatter_about(splits[8], (FF, D), FF ** -0.5, 0.0625, ((0, 8), (1, 16)))
    return {"queries": queries, "keys": keys, "values": values, "span_order": span_order, "ffn_input": ffn_input, "norm_gain": norm_gain, "gate_weight": gate_weight, "up_weight": up_weight, "down_weight": down_weight}


def reference(queries, keys, values, span_order, ffn_input, norm_gain, gate_weight, up_weight, down_weight):
    group_size = H // KVH
    offsets = jnp.arange(TOK_DEV, dtype=jnp.int32)
    positions = (span_order[:, None].astype(jnp.int32) * TOK_DEV + offsets[None, :]).reshape(TOKENS)
    query_pos = positions.reshape(N_CTX, TOK_DEV)
    query_heads = queries.reshape(N_CTX, TOK_DEV, KVH, group_size, HD).transpose(2, 0, 1, 3, 4)
    key_heads = keys.reshape(TOKENS, KVH, HD).transpose(1, 0, 2)
    value_heads = values.reshape(TOKENS, KVH, HD).transpose(1, 0, 2)
    score_scale = 1.0 / math.sqrt(HD)

    def one_head(inputs):
        head_queries, head_keys, head_values = inputs

        def one_block(block):
            block_queries, block_pos = block
            scores = jnp.einsum('qgd,kd->gqk', block_queries.astype(jnp.float32), head_keys.astype(jnp.float32)) * score_scale
            visible = positions[None, :] <= block_pos[:, None]
            scores = jnp.where(visible[None], scores, -1e+30)
            row_max = lax.optimization_barrier(jnp.max(scores, axis=-1))
            weights = jnp.where(visible[None], jnp.exp(scores - row_max[..., None]), 0.0)
            row_sum = lax.optimization_barrier(jnp.sum(weights, axis=-1))
            rounded = lax.optimization_barrier(weights.astype(jnp.bfloat16)).astype(jnp.float32)
            mixed = jnp.einsum('gqk,kd->gqd', rounded, head_values.astype(jnp.float32))
            return ((mixed / row_sum[..., None]).astype(jnp.bfloat16), row_max + jnp.log(row_sum))
        return lax.map(one_block, (head_queries, query_pos))
    outputs, log_parts = lax.map(one_head, (query_heads, key_heads, value_heads))
    attention = outputs.transpose(1, 3, 0, 2, 4).reshape(TOKENS, H * HD)
    log_sums = log_parts.transpose(0, 2, 1, 3).reshape(H, TOKENS)
    widened = ffn_input.astype(jnp.float32)
    mean_sq = lax.optimization_barrier(jnp.mean(widened * widened, axis=-1, keepdims=True))
    normed = (widened * lax.rsqrt(mean_sq + 1e-05) * norm_gain).astype(jnp.bfloat16)
    gate_sum = jnp.dot(normed, gate_weight, preferred_element_type=jnp.float32)
    up_sum = jnp.dot(normed, up_weight, preferred_element_type=jnp.float32)
    hidden = (jax.nn.silu(gate_sum) * up_sum).astype(jnp.bfloat16)
    ffn_out = jnp.dot(hidden, down_weight, preferred_element_type=jnp.float32).astype(jnp.bfloat16)
    return (attention, log_sums, ffn_out)
```

```python
import functools
import math

import jax
import jax.numpy as jnp
from jax import lax
from jax.experimental import pallas as pl
from jax.experimental.pallas import tpu as pltpu
from jax.sharding import PartitionSpec as P

MESH = pl.DeviceIdType.MESH
HD = 128
TOK = 512
BF = jnp.bfloat16
F32 = jnp.float32
KV, GATE, UP, DOWN = range(4)
LOG2E = math.log2(math.e)
SCALE2 = LOG2E / math.sqrt(HD)


def kernel(
    span_ref, gain_ref, q_in, kv_in, f_in, g_in, u_in, d_in,
    att_out, log_out, ffn_out,
    kv_b, g_b, u_b, d_b,
    q_b, f_b, n_b, m_b, acc_b, o_b, orx_b, lg_b, lrx_b,
    ga_b, ua_b, hid_b, ps_b, po_b, rs_b, r_b, rx_b, fs_b, fo_b,
    loc_sem, send_sem, recv_sem, xs_sem, xr_sem,
):
    ctx = lax.axis_index("ctx")
    kvh = lax.axis_index("kvh")
    x, c = kvh // 2, kvh % 2
    y, z = ctx // 4, ctx % 4
    h = y // 2
    same = c * h + (1 - c) * (1 - h)
    is_same = c == h
    not_same = c != h
    yp = y + 1 - 2 * (y % 2)
    yo = 3 - y
    yq = (y + 2) % 4
    yt = same * y + (1 - same) * yo

    def dev(xx, yy, zz, cc):
        return {"ctx": yy * 4 + zz, "kvh": xx * 2 + cc}

    zr, zl, zf = (z + 1) % 4, (z + 3) % 4, (z + 2) % 4
    xr, xl, xf = (x + 1) % 4, (x + 3) % 4, (x + 2) % 4
    SIB = dev(x, y, z, 1 - c)
    PART = dev(x, yp, z, c)
    OPP = dev(x, yo, z, c)
    OPPD = dev(x, yo, z, 1 - c)
    ZR, ZL = dev(x, y, zr, c), dev(x, y, zl, c)
    XR, XL, XF = dev(xr, y, z, c), dev(xl, y, z, c), dev(xf, y, z, c)

    barrier = pltpu.get_barrier_semaphore()
    for t in (SIB, PART, OPP, OPPD, ZR, ZL, XR, XL, XF):
        pl.semaphore_signal(barrier, inc=1, device_id=t, device_id_type=MESH)
    pl.semaphore_wait(barrier, 9)

    sent = []

    def remote(src, dst, ss, rs, target):
        return pltpu.make_async_remote_copy(
            src_ref=src, dst_ref=dst, send_sem=ss, recv_sem=rs,
            device_id=target, device_id_type=MESH,
        )

    bufs = (kv_b, g_b, u_b, d_b)
    ins = (kv_in, g_in, u_in, d_in)
    own = 4 * z + y
    slot_c = same * own + (1 - same) * 16
    yb = (y, yp, yo, yq)
    cps = {}

    def send(a, idx, src, dst, target, go=True):
        cp = remote(src, dst, send_sem.at[a, idx], recv_sem.at[a, idx], target)
        cps[a, idx] = cp
        if go:
            cp.start()
            sent.append(cp)
        return cp

    def block(a, s):
        return bufs[a].at[s, c]

    def pair(a, s):
        return bufs[a].at[pl.ds(s, 2), c]

    def quad(a, s):
        return bufs[a].at[pl.ds(s, 4), c]

    locs = {}

    def start0(a):
        cp = pltpu.make_async_copy(ins[a].at[c], bufs[a].at[slot_c, c], loc_sem.at[a])
        cp.start()
        locs[a] = cp
        send(a, 0, ins[a].at[1 - c], bufs[a].at[slot_c, 1 - c], SIB)

    P0 = 2 * h
    P1 = 2 - 2 * h

    def z_sends(a, b):
        s = 4 * z + yb[b]
        send(a, 4 + b, block(a, s), block(a, s), ZR)
        send(a, 8 + b, block(a, s), block(a, s), ZL)

    def ev(a, n):
        if n == 0:
            locs[a].wait()
            cps[a, 0].wait_recv()
            send(a, 1, block(a, own), block(a, own), PART)
            send(a, 2, block(a, 16), block(a, own), OPP)
            z_sends(a, 0)
        elif n == 1:
            cps[a, 1].wait_recv()
            z_sends(a, 1)
        elif n == 2:
            cps[a, 2].wait_recv()
            s = 4 * z + yo
            send(a, 3, block(a, s), block(a, s), PART)
            z_sends(a, 2)
        elif n == 3:
            cps[a, 3].wait_recv()
            z_sends(a, 3)
            send(a, 14, quad(a, 4 * z), quad(a, 4 * z), SIB)
        elif n == 4:
            cps[a, 4].wait_recv()
            cps[a, 5].wait_recv()
            s = 4 * zl + P0
            send(a, 12, pair(a, s), pair(a, s), ZR)
        elif n == 5:
            cps[a, 10].wait_recv()
            cps[a, 11].wait_recv()
            s = 4 * zr + P1
            send(a, 13, pair(a, s), pair(a, s), ZL)
        elif n == 6:
            cps[a, 6].wait_recv()
            cps[a, 7].wait_recv()
            send(a, 15, quad(a, 4 * zl), quad(a, 4 * zl), SIB)
            cps[a, 8].wait_recv()
            cps[a, 9].wait_recv()
            send(a, 16, quad(a, 4 * zr), quad(a, 4 * zr), SIB)
        elif n == 7:
            cps[a, 12].wait_recv()
            cps[a, 13].wait_recv()
            send(a, 17, quad(a, 4 * zf), quad(a, 4 * zf), SIB)

    def xs(i, src, dst, target):
        return remote(src, dst, xs_sem.at[i], xr_sem.at[i], target)

    k0 = 2 * x + c
    f_loc = pltpu.make_async_copy(f_in, f_b.at[k0], loc_sem.at[4])
    f_sib = xs(0, f_in, f_b.at[k0], SIB)
    f_opp_same = remote(f_in, f_b.at[k0], xs_sem.at[1], xr_sem.at[1 + c], OPP)
    f_opp_diag = remote(f_in, f_b.at[k0], xs_sem.at[1], xr_sem.at[1 + c], OPPD)
    q_loc = pltpu.make_async_copy(q_in, q_b, loc_sem.at[5])
    q_swap = xs(3, q_in, q_b, OPPD)

    @pl.when(is_same)
    def _():
        q_loc.start()
        f_loc.start()
        f_opp_same.start()

    @pl.when(not_same)
    def _():
        q_swap.start()
        f_sib.start()
        f_opp_diag.start()

    def f_wait():
        @pl.when(is_same)
        def _():
            f_loc.wait()
            f_sib.wait_recv()
            f_opp_same.wait_send()

        @pl.when(not_same)
        def _():
            for j in range(2):
                remote(f_in, f_b.at[0], xs_sem.at[1], xr_sem.at[1 + j], OPPD).wait_recv()
            f_opp_diag.wait_send()
            f_sib.wait_send()

    def q_wait():
        @pl.when(is_same)
        def _():
            q_loc.wait()

        @pl.when(not_same)
        def _():
            q_swap.wait()

    fx = {}

    def fev(n):
        if n == 0:
            f_wait()
            mine = f_b.at[pl.ds(2 * x, 2)]
            for i, t in ((4, XR), (5, XL)):
                fx[i] = xs(i, mine, mine, t)
                fx[i].start()
                sent.append(fx[i])
        elif n == 1:
            fx[4].wait_recv()
            one = f_b.at[2 * xl]
            fx[6] = xs(6, one, one, XR)
            fx[6].start()
            sent.append(fx[6])
        elif n == 2:
            fx[5].wait_recv()
            one = f_b.at[2 * xr + 1]
            fx[7] = xs(7, one, one, XL)
            fx[7].start()
            sent.append(fx[7])
        elif n == 3:
            fx[6].wait_recv()
            fx[7].wait_recv()

    events = []

    def add(*names):
        for nm in names:
            a, n = nm[0], int(nm[1:])
            if a == "F":
                events.append((nm, functools.partial(fev, n)))
            else:
                events.append((nm, functools.partial(ev, "KGUD".index(a), n)))

    add("K0", "F0", "G0", "K1", "K2", "K3", "G1", "K4", "K5", "G2", "K6", "G3", "U0", "K7")
    add("U1", "G4", "F1", "U2", "G5", "F2", "U3", "G6", "F3", "D0", "G7", "U4", "U5", "U6")
    add("D1", "D2", "D3", "U7", "D4", "D5", "D6", "D7")
    done = set()
    at = [0]

    def pump(count):
        for _ in range(count):
            if at[0] < len(events):
                nm, fn = events[at[0]]
                fn()
                done.add(nm)
                at[0] += 1

    def until(nm):
        while nm not in done:
            pump(1)

    groups = (z, zl, zr, zf)
    ready = ("3", "6", "6", "7")

    def group_ready(a, i):
        until("KGUD"[a] + ready[i])
        cps[a, 14 + i].wait_recv()

    start0(KV)
    start0(GATE)
    start0(UP)
    start0(DOWN)

    my_span = span_ref[yt * 4 + z]

    def attend(slot, src, first):
        visible = (span_ref[src] < my_span).astype(F32)
        hide = (1.0 - visible) * 1e30

        def head(g, _):
            k = kv_b[slot, 0]
            v = kv_b[slot, 1]
            va = jnp.concatenate([v, jnp.ones((TOK, HD), BF)], axis=1)
            col = pl.multiple_of(g * HD, HD)
            for t in range(2):
                rows = pl.ds(t * 256, 256)
                q = q_b[rows, pl.ds(col, HD)]
                s = lax.dot_general(q, k, (((1,), (1,)), ((), ())), preferred_element_type=F32)
                if first:
                    ri = lax.broadcasted_iota(jnp.int32, (256, TOK), 0) + t * 256
                    ci = lax.broadcasted_iota(jnp.int32, (256, TOK), 1)
                    s = jnp.where(ci <= ri, s, -1e30)
                    top = jnp.broadcast_to(jnp.max(s, axis=1, keepdims=True), (256, HD))
                    m_new = top * SCALE2
                    p = jnp.exp2(s * SCALE2 - jnp.concatenate([m_new] * 4, axis=1))
                    acc_b[g, rows] = jnp.dot(p.astype(BF), va, preferred_element_type=F32)
                else:
                    top = jnp.broadcast_to(jnp.max(s, axis=1, keepdims=True), (256, HD))
                    m_old = m_b[g, rows]
                    m_new = jnp.maximum(m_old, top * SCALE2 - hide)
                    alpha = jnp.exp2(m_old - m_new)
                    sub = m_new + hide
                    p = jnp.exp2(s * SCALE2 - jnp.concatenate([sub] * 4, axis=1))
                    pv = jnp.dot(p.astype(BF), va, preferred_element_type=F32)
                    acc_b[g, rows] = acc_b[g, rows] * jnp.concatenate([alpha] * 2, axis=1) + pv
                m_b[g, rows] = m_new
            return 0

        lax.fori_loop(0, 4, head, 0)

    def attend_group(i, pumps):
        group_ready(KV, i)
        zs = groups[i]
        for j in range(4):
            ys = (yt + j) % 4
            attend(4 * zs + ys, ys * 4 + zs, i == 0 and j == 0)
            pump(pumps)

    until("K3")
    q_wait()
    attend_group(0, 1)
    attend_group(1, 1)
    attend_group(2, 1)
    attend_group(3, 1)

    def finish(g, _):
        col = pl.multiple_of(g * HD, HD)
        total = acc_b[g, :, HD:]
        o_b[:, pl.ds(col, HD)] = (acc_b[g, :, :HD] / total).astype(BF)
        logs = m_b[g] * (1.0 / LOG2E) + jnp.log(total)
        lg_b[g] = jnp.transpose(logs)[:8]
        return 0

    lax.fori_loop(0, 4, finish, 0)
    o_swap = xs(8, o_b, orx_b, OPPD)
    l_swap = xs(9, lg_b, lrx_b, OPPD)

    @pl.when(is_same)
    def _():
        att_out[...] = o_b[...]
        for g in range(4):
            log_out[pl.ds(g, 1)] = lg_b[g, :1]

    @pl.when(not_same)
    def _():
        o_swap.start()
        l_swap.start()

    until("F3")

    def norm(i, _):
        rows = pl.ds(i * 64, 64)
        part = jnp.zeros((64, TOK), F32)
        for k in range(8):
            v = f_b[k, rows].astype(F32)
            part = part + v * v
        r = lax.rsqrt(jnp.sum(part, axis=1, keepdims=True) * (1.0 / 4096) + 1e-05)
        for k in range(8):
            n_b[k, rows] = (f_b[k, rows].astype(F32) * r * gain_ref[pl.ds(k, 1)]).astype(BF)
        return 0

    lax.fori_loop(0, 8, norm, 0)

    def project(a, i):
        group_ready(a, i)
        zs = groups[i]
        out = ga_b if a == GATE else ua_b
        off = pl.multiple_of((zs % 2) * 256, 256)

        def rows_of(t, _):
            rows = pl.ds(t * 256, 256)
            lhs = jnp.concatenate(
                [n_b[2 * ys + zs // 2, rows, pl.ds(off, 256)] for ys in range(4)], axis=1
            )
            w = bufs[a][pl.ds(4 * zs, 4)].reshape(1024, 896)
            res = jnp.dot(lhs, w, preferred_element_type=F32)
            if i == 0:
                out[rows] = res
            else:
                out[rows] = out[rows] + res
            return 0

        lax.fori_loop(0, 2, rows_of, 0)

    for i in range(4):
        project(GATE, i)
    for i in range(4):
        project(UP, i)

    def act(i, _):
        rows = pl.ds(i * 64, 64)
        g = ga_b[rows]
        hid_b[rows] = (g / (1.0 + jnp.exp(-g)) * ua_b[rows]).astype(BF)
        return 0

    lax.fori_loop(0, 8, act, 0)

    rel = ((2, xf, XF), (0, xr, XR), (1, xl, XL))
    rsc = {}

    def down(i):
        group_ready(DOWN, i)
        zs = groups[i]
        for n, xd, target in rel:
            w = d_b[4 * zs + xd].reshape(896, 256)
            ps_b[i, n] = jnp.dot(hid_b[...], w, preferred_element_type=F32).astype(BF)
            cp = xs(10 + 3 * i + n, ps_b.at[i, n], rs_b.at[i, n], target)
            cp.start()
            sent.append(cp)
            rsc[i, n] = cp
        w = d_b[4 * zs + x].reshape(896, 256)
        po_b[i] = jnp.dot(hid_b[...], w, preferred_element_type=F32)

    tail = []

    def combine(i):
        zs = groups[i]
        for n in range(3):
            rsc[i, n].wait_recv()
        to_opp = xs(22 + i, r_b.at[i], rx_b.at[i], OPP)
        total = po_b[i]
        for n in range(3):
            total = total + rs_b[i, n].astype(F32)
        po_b[i] = total

        @pl.when(not_same)
        def _():
            r_b[i] = po_b[i].astype(BF)
            to_opp.start()

        tail.append(to_opp)

    def close(i):
        zs = groups[i]
        sub = zs % 2
        here = zs // 2 == c
        off = pl.multiple_of(sub * 256, 256)
        to_sib = remote(fs_b.at[i], fo_b.at[sub], xs_sem.at[26 + i], xr_sem.at[26 + sub], SIB)

        @pl.when(is_same)
        def _():
            tail[i].wait_recv()
            res = (po_b[i] + rx_b[i].astype(F32)).astype(BF)

            @pl.when(here)
            def _():
                ffn_out[:, pl.ds(off, 256)] = res

            @pl.when(zs // 2 != c)
            def _():
                fs_b[i] = res
                to_sib.start()

        return to_sib

    sibs = []
    down(0)
    down(1)
    combine(0)
    down(2)
    combine(1)
    sibs.append(close(0))
    down(3)
    combine(2)
    sibs.append(close(1))
    combine(3)
    sibs.append(close(2))
    sibs.append(close(3))

    @pl.when(is_same)
    def _():
        for i in range(4):
            @pl.when(groups[i] // 2 != c)
            def _():
                sibs[i].wait_send()

    @pl.when(not_same)
    def _():
        o_swap.wait()
        l_swap.wait()
        att_out[...] = orx_b[...]
        for g in range(4):
            log_out[pl.ds(g, 1)] = lrx_b[g, :1]
        for i in range(4):
            tail[i].wait_send()
        for s in range(2):
            remote(fs_b.at[0], fo_b.at[s], xs_sem.at[26], xr_sem.at[26 + s], SIB).wait_recv()
            ffn_out[:, s * 256 : (s + 1) * 256] = fo_b[s]

    for cp in sent:
        cp.wait_send()


def body(queries, keys, values, span_order, ffn_input, norm_gain, gate_w, up_w, down_w):
    anyspace = pl.BlockSpec(memory_space=pl.ANY)
    vmem = pl.BlockSpec(memory_space=pltpu.VMEM)
    smem = pl.BlockSpec(memory_space=pltpu.SMEM)
    sem = pltpu.SemaphoreType.DMA
    return pl.pallas_call(
        kernel,
        out_shape=(
            jax.ShapeDtypeStruct((512, 512), BF),
            jax.ShapeDtypeStruct((4, 512), F32),
            jax.ShapeDtypeStruct((512, 512), BF),
        ),
        in_specs=[smem, vmem] + [anyspace] * 6,
        out_specs=(vmem, vmem, vmem),
        scratch_shapes=[
            pltpu.VMEM((17, 2, 512, 128), BF),
            pltpu.VMEM((17, 2, 128, 896), BF),
            pltpu.VMEM((17, 2, 128, 896), BF),
            pltpu.VMEM((17, 2, 448, 256), BF),
            pltpu.VMEM((512, 512), BF),
            pltpu.VMEM((8, 512, 512), BF),
            pltpu.VMEM((8, 512, 512), BF),
            pltpu.VMEM((4, 512, 128), F32),
            pltpu.VMEM((4, 512, 256), F32),
            pltpu.VMEM((512, 512), BF),
            pltpu.VMEM((512, 512), BF),
            pltpu.VMEM((4, 8, 512), F32),
            pltpu.VMEM((4, 8, 512), F32),
            pltpu.VMEM((512, 896), F32),
            pltpu.VMEM((512, 896), F32),
            pltpu.VMEM((512, 896), BF),
            pltpu.VMEM((4, 3, 512, 256), BF),
            pltpu.VMEM((4, 512, 256), F32),
            pltpu.VMEM((4, 3, 512, 256), BF),
            pltpu.VMEM((4, 512, 256), BF),
            pltpu.VMEM((4, 512, 256), BF),
            pltpu.VMEM((4, 512, 256), BF),
            pltpu.VMEM((2, 512, 256), BF),
            sem((6,)),
            sem((4, 18)),
            sem((4, 18)),
            sem((30,)),
            sem((30,)),
        ],
        compiler_params=pltpu.CompilerParams(
            collective_id=0, has_side_effects=True, vmem_limit_bytes=62 * 2**20
        ),
        name="layer",
    )(
        span_order,
        norm_gain.reshape(8, 512),
        queries,
        jnp.stack([keys, values]),
        ffn_input,
        gate_w.reshape(2, 128, 896),
        up_w.reshape(2, 128, 896),
        down_w.reshape(2, 448, 256),
    )


def solution(mesh):
    placed = (
        P("ctx", "kvh"), P("ctx", "kvh"), P("ctx", "kvh"), P(), P("ctx", "kvh"), P(),
        P("ctx", "kvh"), P("ctx", "kvh"), P("kvh", "ctx"),
    )
    return jax.shard_map(
        body,
        mesh=mesh,
        in_specs=placed,
        out_specs=(P("ctx", "kvh"), P("kvh", "ctx"), P("ctx", "kvh")),
        check_vma=False,
    )
```

```python
import functools
import math

import jax
import jax.numpy as jnp
from jax import lax
from jax.experimental import pallas as pl
from jax.experimental.pallas import tpu as pltpu
from jax.sharding import PartitionSpec as P

MESH = pl.DeviceIdType.MESH
HD = 128
TOK = 512
BF = jnp.bfloat16
F32 = jnp.float32
KV, GATE, UP, DOWN = range(4)
LOG2E = math.log2(math.e)
SCALE2 = LOG2E / math.sqrt(HD)

ORDER = (
    "st", "K0", "F0a", "G0", "U0", "K1", "Fs", "Q", "K2", "G1", "G2", "F1a", "F2a", "K3", "U4",
    "U1", "U2", "Kr0", "A00", "G3", "K4", "A01", "A02", "A03", "U8", "Gr0", "F0b", "G4", "Ur0",
    "U5", "K5", "K6", "U6", "Kr1", "A10", "U3", "U9", "F1b", "F2b", "Kr2", "A11", "A12", "U10",
    "A13", "Ur1", "G5", "G6", "A20", "U7", "A21", "Ur2", "F3", "D0", "K7", "N", "Gr1", "PG0", "Gr2",
    "Kr3", "PG1", "U11", "PG2", "D2", "PU0", "G7", "D1", "PU1", "Ur3", "PU2", "PU3", "Gr3", "D3",
    "PG3", "ACT", "A22", "Dr0", "W02", "W00", "W01", "W03", "A23", "D4", "A30", "X00", "X01", "A31",
    "D5", "D6", "A32", "A33", "C0", "AF", "Dr1", "W12", "W10", "W11", "Dr2", "W22", "W20", "W21",
    "E0", "W13", "W23", "X10", "X11", "D7", "X20", "Dr3", "X21", "W32", "W30", "W31", "W33", "C1",
    "C2", "E1", "X30", "X31", "E2", "C3", "E3",
)


def kernel(
    span_ref, gain_ref, q_in, kv_in, f_in, g_in, u_in, d_in,
    att_out, log_out, ffn_out,
    kv_b, g_b, u_b, d_b,
    q_b, f_b, n_b, m_b, acc_b, o_b, orx_b, lg_b, lrx_b,
    ga_b, ua_b, hid_b, ps_b, po_b, fr_b, rs_b, r_b, rx_b, fs_b, fo_b,
    loc_sem, send_sem, recv_sem, xs_sem, xr_sem,
):
    ctx = lax.axis_index("ctx")
    kvh = lax.axis_index("kvh")
    x, c = kvh // 2, kvh % 2
    y, z = ctx // 4, ctx % 4
    h = y // 2
    same = c * h + (1 - c) * (1 - h)
    is_same = c == h
    not_same = c != h
    yp = y + 1 - 2 * (y % 2)
    yo = 3 - y
    yq = (y + 2) % 4
    yt = same * y + (1 - same) * yo

    def dev(xx, yy, zz, cc):
        return {"ctx": yy * 4 + zz, "kvh": xx * 2 + cc}

    zr, zl, zf = (z + 1) % 4, (z + 3) % 4, (z + 2) % 4
    xr, xl = (x + 1) % 4, (x + 3) % 4
    SIB = dev(x, y, z, 1 - c)
    PART = dev(x, yp, z, c)
    OPP = dev(x, yo, z, c)
    OPPD = dev(x, yo, z, 1 - c)
    ZR, ZL = dev(x, y, zr, c), dev(x, y, zl, c)
    XR, XL = dev(xr, y, z, c), dev(xl, y, z, c)

    barrier = pltpu.get_barrier_semaphore()
    for t in (SIB, PART, OPP, OPPD, ZR, ZL, XR, XL):
        pl.semaphore_signal(barrier, inc=1, device_id=t, device_id_type=MESH)
    pl.semaphore_wait(barrier, 8)

    def remote(src, dst, ss, rs, target):
        return pltpu.make_async_remote_copy(
            src_ref=src, dst_ref=dst, send_sem=ss, recv_sem=rs,
            device_id=target, device_id_type=MESH,
        )

    bufs = (kv_b, g_b, u_b, d_b)
    ins = (kv_in, g_in, u_in, d_in)
    groups = (z, zl, zr, zf)
    own = 4 * z + y
    extra = (16, 16, 16 + z, 16)
    yb = (y, yp, yo, yq)
    P0 = 2 * h
    P1 = 2 - 2 * h
    sent = {}

    def copy_of(a, idx):
        def cp(s, d, target, count=1):
            if count == 1:
                src, dst = bufs[a].at[s, c], bufs[a].at[d, c]
            else:
                src = bufs[a].at[pl.ds(s, count), c]
                dst = bufs[a].at[pl.ds(d, count), c]
            return remote(src, dst, send_sem.at[a, idx], recv_sem.at[a, idx], target)

        if idx == 0:
            slot = same * own + (1 - same) * extra[a]
            return remote(
                ins[a].at[1 - c], bufs[a].at[slot, 1 - c],
                send_sem.at[a, 0], recv_sem.at[a, 0], SIB,
            )
        if 14 <= idx < 18:
            s = 4 * groups[idx - 14]
            return cp(s, s, SIB, 4)
        if a == UP:
            if idx in (4, 6):
                return cp(own, own, ZR if idx == 4 else ZL)
            if idx in (5, 7):
                return cp(16 + z, 16 + z, ZR if idx == 5 else ZL)
            if idx == 8:
                return cp(4 * zl + y, 4 * zl + y, ZR)
            if idx == 9:
                return cp(16 + zr, 16 + zr, ZL)
            zs = groups[idx % 4]
            if 20 <= idx < 24:
                return cp(4 * zs + y, 4 * zs + y, PART)
            if 24 <= idx < 28:
                return cp(16 + zs, 4 * zs + y, OPP)
            return cp(4 * zs + yo, 4 * zs + yo, PART)
        if idx == 1:
            return cp(own, own, PART)
        if idx == 2:
            return cp(16, own, OPP)
        if idx == 3:
            return cp(4 * z + yo, 4 * z + yo, PART)
        if 4 <= idx < 12:
            s = 4 * z + yb[idx % 4]
            return cp(s, s, ZR if idx < 8 else ZL)
        if idx == 12:
            return cp(4 * zl + P0, 4 * zl + P0, ZR, 2)
        return cp(4 * zr + P1, 4 * zr + P1, ZL, 2)

    def local_of(a):
        slot = same * own + (1 - same) * extra[a]
        return pltpu.make_async_copy(ins[a].at[c], bufs[a].at[slot, c], loc_sem.at[a])

    def go(a, *idxs):
        for idx in idxs:
            copy_of(a, idx).start()
            sent[a, idx] = True

    def got(a, *idxs):
        for idx in idxs:
            copy_of(a, idx).wait_recv()

    def ev_z(a, n):
        if n == 0:
            local_of(a).wait()
            got(a, 0)
            go(a, 1, 2, 4, 8)
        elif n == 1:
            got(a, 1)
            go(a, 5, 9)
        elif n == 2:
            got(a, 2)
            go(a, 3, 6, 10)
        elif n == 3:
            got(a, 3)
            go(a, 7, 11, 14)
        elif n == 4:
            got(a, 4, 5)
            go(a, 12)
        elif n == 5:
            got(a, 10, 11)
            go(a, 13)
        elif n == 6:
            got(a, 6, 7)
            go(a, 15)
            got(a, 8, 9)
            go(a, 16)
        elif n == 7:
            got(a, 12, 13)
            go(a, 17)

    def ev_y(a, n):
        if n == 0:
            local_of(a).wait()
            got(a, 0)
            go(a, 4, 7, 5, 6, 20, 24)
        elif n == 1:
            got(a, 4, 5)
            go(a, 8, 21, 25)
        elif n == 2:
            got(a, 6, 7)
            go(a, 9, 22, 26)
        elif n == 3:
            got(a, 8, 9)
            go(a, 23, 27)
        elif n < 8:
            got(a, 20 + n)
            go(a, 24 + n)
        else:
            got(a, 12 + n, 20 + n)
            go(a, 6 + n)

    k0 = 2 * x + c
    two = pl.ds(2 * x, 2)

    def xc(i, j=0):
        def cp(src, dst, target):
            return remote(src, dst, xs_sem.at[i], xr_sem.at[i], target)

        if i == 0:
            return cp(f_in, f_b.at[k0], SIB)
        if i in (1, 2):
            return remote(
                f_in, f_b.at[k0], xs_sem.at[1], xr_sem.at[1 + c], OPP if i == 1 else OPPD
            )
        if i == 3:
            return cp(q_in, q_b, OPPD)
        if i in (4, 5):
            return cp(f_b.at[two], f_b.at[two], XR if i == 4 else XL)
        if i == 6:
            return cp(f_b.at[2 * xl], f_b.at[2 * xl], XR)
        if i == 7:
            return cp(f_b.at[2 * xr + 1], f_b.at[2 * xr + 1], XL)
        if i == 8:
            return cp(o_b, orx_b, OPPD)
        if i == 9:
            return cp(lg_b, lrx_b, OPPD)
        if i < 14:
            return cp(r_b.at[i - 10], rx_b.at[i - 10], OPP)
        if i < 18:
            n = i - 14
            sub = groups[n] % 2
            return remote(fs_b.at[n], fo_b.at[sub], xs_sem.at[i], xr_sem.at[14 + sub], SIB)
        g, n = (i - 18) // 6, (i - 18) % 6
        lo, hi = pl.ds(0, 256), pl.ds(256, 256)
        if n == 0:
            return cp(ps_b.at[g, 2, lo], fr_b.at[g, 0], XR)
        if n == 1:
            return cp(ps_b.at[g, 2, hi], fr_b.at[g, 1], XL)
        if n == 2:
            return cp(ps_b.at[g, 0, hi], rs_b.at[g, 0, hi], XR)
        if n == 3:
            return cp(ps_b.at[g, 1, lo], rs_b.at[g, 1, lo], XL)
        if n == 4:
            return cp(ps_b.at[g, 0, lo], rs_b.at[g, 0, lo], XR)
        return cp(ps_b.at[g, 1, hi], rs_b.at[g, 1, hi], XL)

    f_loc = pltpu.make_async_copy(f_in, f_b.at[k0], loc_sem.at[4])
    q_loc = pltpu.make_async_copy(q_in, q_b, loc_sem.at[5])

    def start():
        @pl.when(is_same)
        def _():
            f_loc.start()
            q_loc.start()

        @pl.when(not_same)
        def _():
            xc(0).start()
            xc(3).start()

        for a in (KV, GATE, UP, DOWN):
            local_of(a).start()
            go(a, 0)

    def feat(nm):
        if nm == "Fs":
            pl.when(is_same)(lambda: xc(1).start())
            pl.when(not_same)(lambda: xc(2).start())
            return
        n = nm[1]
        if n == "3":
            xc(6).wait_recv()
            xc(7).wait_recv()
            return

        @pl.when(is_same if nm[2] == "a" else not_same)
        def _():
            if nm == "F0a":
                f_loc.wait()
                xc(0).wait_recv()
            elif nm == "F0b":
                for j in range(2):
                    remote(f_in, f_b.at[0], xs_sem.at[1], xr_sem.at[1 + j], OPP).wait_recv()
            if n == "0":
                xc(4).start()
                xc(5).start()
            elif n == "1":
                xc(4).wait_recv()
                xc(6).start()
            else:
                xc(5).wait_recv()
                xc(7).start()

    def q_wait():
        pl.when(is_same)(lambda: q_loc.wait())
        pl.when(not_same)(lambda: xc(3).wait())

    my_span = span_ref[yt * 4 + z]

    def attend(slot, src, first):
        hide = jnp.where(span_ref[src] < my_span, 0.0, 1e30).astype(F32)
        k = kv_b[slot, 0]
        va = jnp.concatenate([kv_b[slot, 1], jnp.ones((TOK, HD), BF)], axis=1)
        step = 128
        for g in range(4):
            for t in range(TOK // step):
                rows = slice(t * step, t * step + step)
                q = q_b[rows, g * HD : g * HD + HD]
                s = lax.dot_general(q, k, (((1,), (1,)), ((), ())), preferred_element_type=F32)
                if first:
                    ri = lax.broadcasted_iota(jnp.int32, (step, TOK), 0) + t * step
                    ci = lax.broadcasted_iota(jnp.int32, (step, TOK), 1)
                    s = jnp.where(ci <= ri, s, -1e30)
                    m_new = jnp.broadcast_to(jnp.max(s, axis=1, keepdims=True), (step, HD)) * SCALE2
                    p = jnp.exp2(s * SCALE2 - jnp.concatenate([m_new] * 4, axis=1))
                    acc_b[g, rows] = jnp.dot(p.astype(BF), va, preferred_element_type=F32)
                else:
                    m_old = m_b[g, rows]
                    top = jnp.max(s, axis=1, keepdims=True) * SCALE2 - hide
                    m_new = jnp.maximum(m_old, top)
                    alpha = jnp.exp2(m_old - m_new)
                    sub = m_new + hide
                    p = jnp.exp2(s * SCALE2 - jnp.concatenate([sub] * 4, axis=1))
                    pv = jnp.dot(p.astype(BF), va, preferred_element_type=F32)
                    acc_b[g, rows] = acc_b[g, rows] * jnp.concatenate([alpha] * 2, axis=1) + pv
                m_b[g, rows] = m_new

    def finish():
        for g in range(4):
            col = g * HD
            total = acc_b[g, :, HD:]
            o_b[:, col : col + HD] = (acc_b[g, :, :HD] / total).astype(BF)
            logs = m_b[g] * (1.0 / LOG2E) + jnp.log(total)
            lg_b[g] = jnp.transpose(logs)[:8]

        @pl.when(is_same)
        def _():
            att_out[...] = o_b[...]
            for g in range(4):
                log_out[pl.ds(g, 1)] = lg_b[g, :1]

        @pl.when(not_same)
        def _():
            xc(8).start()
            xc(9).start()

    def norm():
        def rows_of(i, _):
            rows = pl.ds(i * 64, 64)
            part = jnp.zeros((64, TOK), F32)
            for k in range(8):
                v = f_b[k, rows].astype(F32)
                part = part + v * v
            r = lax.rsqrt(jnp.sum(part, axis=1, keepdims=True) * (1.0 / 4096) + 1e-05)
            for k in range(8):
                n_b[k, rows] = (f_b[k, rows].astype(F32) * r * gain_ref[pl.ds(k, 1)]).astype(BF)
            return 0

        lax.fori_loop(0, 8, rows_of, 0)

    def project(a, i):
        zs = groups[i]
        out = ga_b if a == GATE else ua_b
        off = pl.multiple_of((zs % 2) * 256, 256)

        def rows_of(t, _):
            rows = pl.ds(t * 256, 256)
            lhs = jnp.concatenate(
                [n_b[2 * ys + zs // 2, rows, pl.ds(off, 256)] for ys in range(4)], axis=1
            )
            w = bufs[a][pl.ds(4 * zs, 4)].reshape(1024, 896)
            res = jnp.dot(lhs, w, preferred_element_type=F32)
            if i == 0:
                out[rows] = res
            else:
                out[rows] = out[rows] + res
            return 0

        lax.fori_loop(0, 2, rows_of, 0)

    def act():
        def rows_of(i, _):
            rows = pl.ds(i * 64, 64)
            g = ga_b[rows]
            hid_b[rows] = (g / (1.0 + jnp.exp(-g)) * ua_b[rows]).astype(BF)
            return 0

        lax.fori_loop(0, 8, rows_of, 0)

    def x_go(i, *ns):
        for n in ns:
            xc(18 + 6 * i + n).start()
            sent[18 + 6 * i + n] = True

    def x_got(i, *ns):
        for n in ns:
            xc(18 + 6 * i + n).wait_recv()

    def down(i, n):
        xd = (xr, xl, (x + 2) % 4, x)[n]
        w = d_b[4 * groups[i] + xd].reshape(896, 256)
        res = jnp.dot(hid_b[...], w, preferred_element_type=F32)
        if n == 3:
            po_b[i] = res
            return
        ps_b[i, n] = res.astype(BF)
        if n == 2:
            x_go(i, 0, 1)
        else:
            x_go(i, 2 + n)

    def forward(i, n):
        x_got(i, n)
        rows = pl.ds(256 * n, 256)
        ps_b[i, n, rows] = (ps_b[i, n, rows].astype(F32) + fr_b[i, n].astype(F32)).astype(BF)
        x_go(i, 4 + n)

    def combine(i):
        x_got(i, 2, 3, 4, 5)
        po_b[i] = po_b[i] + rs_b[i, 0].astype(F32) + rs_b[i, 1].astype(F32)

        @pl.when(not_same)
        def _():
            r_b[i] = po_b[i].astype(BF)
            xc(10 + i).start()

    def close(i):
        zs = groups[i]
        off = pl.multiple_of((zs % 2) * 256, 256)

        @pl.when(is_same)
        def _():
            xc(10 + i).wait_recv()
            res = (po_b[i] + rx_b[i].astype(F32)).astype(BF)

            @pl.when(zs // 2 == c)
            def _():
                ffn_out[:, pl.ds(off, 256)] = res

            @pl.when(zs // 2 != c)
            def _():
                fs_b[i] = res
                xc(14 + i).start()

    def run(nm):
        if nm == "st":
            start()
        elif nm[0] == "F":
            feat(nm)
        elif nm == "Q":
            q_wait()
        elif nm == "AF":
            finish()
        elif nm == "N":
            norm()
        elif nm == "ACT":
            act()
        elif nm[0] == "P":
            project("KGUD".index(nm[1]), int(nm[2]))
        elif nm[0] == "W":
            down(int(nm[1]), int(nm[2]))
        elif nm[0] == "X":
            forward(int(nm[1]), int(nm[2]))
        elif nm[0] == "C":
            combine(int(nm[1]))
        elif nm[0] == "E":
            close(int(nm[1]))
        else:
            a = "KGUD".index(nm[0])
            if nm[1] == "r":
                got(a, 14 + int(nm[2]))
            elif a == UP:
                ev_y(a, int(nm[1:]))
            else:
                ev_z(a, int(nm[1:]))

    parts = [[]]
    for nm in ORDER:
        if nm[0] == "A" and nm[1:].isdigit():
            parts.append([])
        else:
            parts[-1].append(nm)
    for nm in parts[0]:
        run(nm)
    attend(4 * z + yt, yt * 4 + z, True)
    for nm in parts[1]:
        run(nm)

    def block(n, _):
        i, j = n // 4, n % 4
        delta = (i // 2) * (i - 1) + (1 - i // 2) * (3 * i)
        zs = (z + delta) % 4
        ys = (yt + j) % 4
        attend(4 * zs + ys, ys * 4 + zs, False)
        for m in range(1, 15):
            if parts[m + 1]:
                @pl.when(n == m)
                def _():
                    for nm in parts[m + 1]:
                        run(nm)
        return 0

    lax.fori_loop(1, 16, block, 0)
    for nm in parts[16]:
        run(nm)

    @pl.when(is_same)
    def _():
        xc(1).wait_send()
        for i in range(4):
            pl.when(groups[i] // 2 != c)(lambda: xc(14 + i).wait_send())

    @pl.when(not_same)
    def _():
        xc(0).wait_send()
        xc(2).wait_send()
        xc(8).wait()
        xc(9).wait()
        att_out[...] = orx_b[...]
        for g in range(4):
            log_out[pl.ds(g, 1)] = lrx_b[g, :1]
        for i in range(4):
            xc(10 + i).wait_send()
        for s in range(2):
            remote(fs_b.at[0], fo_b.at[s], xs_sem.at[14], xr_sem.at[14 + s], SIB).wait_recv()
            ffn_out[:, s * 256 : (s + 1) * 256] = fo_b[s]

    for i in (4, 5, 6, 7):
        xc(i).wait_send()
    for it in sent:
        if isinstance(it, tuple):
            copy_of(*it).wait_send()
        else:
            xc(it).wait_send()


def body(queries, keys, values, span_order, ffn_input, norm_gain, gate_w, up_w, down_w):
    anyspace = pl.BlockSpec(memory_space=pl.ANY)
    vmem = pl.BlockSpec(memory_space=pltpu.VMEM)
    smem = pl.BlockSpec(memory_space=pltpu.SMEM)
    sem = pltpu.SemaphoreType.DMA
    return pl.pallas_call(
        kernel,
        out_shape=(
            jax.ShapeDtypeStruct((512, 512), BF),
            jax.ShapeDtypeStruct((4, 512), F32),
            jax.ShapeDtypeStruct((512, 512), BF),
        ),
        in_specs=[smem, vmem] + [anyspace] * 6,
        out_specs=(vmem, vmem, vmem),
        scratch_shapes=[
            pltpu.VMEM((17, 2, 512, 128), BF),
            pltpu.VMEM((17, 2, 128, 896), BF),
            pltpu.VMEM((20, 2, 128, 896), BF),
            pltpu.VMEM((17, 2, 448, 256), BF),
            pltpu.VMEM((512, 512), BF),
            pltpu.VMEM((8, 512, 512), BF),
            pltpu.VMEM((8, 512, 512), BF),
            pltpu.VMEM((4, 512, 128), F32),
            pltpu.VMEM((4, 512, 256), F32),
            pltpu.VMEM((512, 512), BF),
            pltpu.VMEM((512, 512), BF),
            pltpu.VMEM((4, 8, 512), F32),
            pltpu.VMEM((4, 8, 512), F32),
            pltpu.VMEM((512, 896), F32),
            pltpu.VMEM((512, 896), F32),
            pltpu.VMEM((512, 896), BF),
            pltpu.VMEM((4, 3, 512, 256), BF),
            pltpu.VMEM((4, 512, 256), F32),
            pltpu.VMEM((4, 2, 256, 256), BF),
            pltpu.VMEM((4, 2, 512, 256), BF),
            pltpu.VMEM((4, 512, 256), BF),
            pltpu.VMEM((4, 512, 256), BF),
            pltpu.VMEM((4, 512, 256), BF),
            pltpu.VMEM((2, 512, 256), BF),
            sem((6,)),
            sem((4, 32)),
            sem((4, 32)),
            sem((42,)),
            sem((42,)),
        ],
        compiler_params=pltpu.CompilerParams(
            collective_id=0, has_side_effects=True, vmem_limit_bytes=63 * 2**20
        ),
        name="layer",
    )(
        span_order,
        norm_gain.reshape(8, 512),
        queries,
        jnp.stack([keys, values]),
        ffn_input,
        gate_w.reshape(2, 128, 896),
        up_w.reshape(2, 128, 896),
        down_w.reshape(2, 448, 256),
    )


def solution(mesh):
    placed = (
        P("ctx", "kvh"), P("ctx", "kvh"), P("ctx", "kvh"), P(), P("ctx", "kvh"), P(),
        P("ctx", "kvh"), P("ctx", "kvh"), P("kvh", "ctx"),
    )
    return jax.shard_map(
        body,
        mesh=mesh,
        in_specs=placed,
        out_specs=(P("ctx", "kvh"), P("kvh", "ctx"), P("ctx", "kvh")),
        check_vma=False,
    )
```

```python
import functools
import math

import jax
import jax.numpy as jnp
from jax import lax
from jax.experimental import pallas as pl
from jax.experimental.pallas import tpu as pltpu
from jax.sharding import PartitionSpec as P

MESH = pl.DeviceIdType.MESH
HD = 128
TOK = 512
BF = jnp.bfloat16
F32 = jnp.float32
KV, GATE, UP, DOWN = range(4)
LOG2E = math.log2(math.e)
SCALE2 = LOG2E / math.sqrt(HD)

ORDER = (
    "st", "K0", "F0a", "G0", "U0", "K4", "G1", "G2", "Fs", "F1a", "U4", "K8", "Kr0", "G3", "U1",
    "U2", "Q", "Gr0", "U8", "G4", "F2a", "F0b", "U5", "G5", "G6", "U6", "Gr1", "U3", "U9", "Gr2",
    "D0", "F2b", "F1b", "U10", "Ur1", "A00", "A01", "U7", "A02", "Ur2", "G7", "A03", "D2", "F3",
    "Ur0", "K1", "N", "D1", "Gr3", "PU0", "PU2", "K5", "K2", "PU1", "U11", "PG0", "PG3", "PG1",
    "K6", "D3", "Ur3", "PU3", "PG2", "K3", "D4", "ACT", "Dr0", "W02", "W01", "K9", "W03", "W00",
    "D5", "D6", "K7", "Kr1", "A10", "X01", "X00", "K10", "A11", "Dr1", "W10", "W11", "W12", "A12",
    "Dr2", "W21", "W23", "Kr2", "C0", "K11", "W20", "W22", "A13", "D7", "A20", "X10", "E0", "X11",
    "Kr3", "A21", "A22", "Dr3", "W33", "W32", "W30", "A23", "X21", "X20", "A30", "W13", "C1", "A31",
    "X30", "W31", "X31", "A32", "A33", "E1", "AF", "C2", "C3", "E2", "E3",
)


def kernel(
    span_ref, gain_ref, q_in, k_in, v_in, f_in, g_in, u_in, d_in,
    att_out, log_out, ffn_out,
    kv_b, g_b, u_b, d_b,
    q_b, f_b, n_b, m_b, acc_b, o_b, orx_b, lg_b, lrx_b,
    ga_b, ua_b, hid_b, ps_b, po_b, fr_b, rs_b, r_b, rx_b, fo_b,
    loc_sem, send_sem, recv_sem, xs_sem, xr_sem,
):
    ctx = lax.axis_index("ctx")
    kvh = lax.axis_index("kvh")
    x, c = kvh // 2, kvh % 2
    y, z = ctx // 4, ctx % 4
    h = y // 2
    same = c * h + (1 - c) * (1 - h)
    is_same = c == h
    not_same = c != h
    yp = y + 1 - 2 * (y % 2)
    yo = 3 - y
    yq = (y + 2) % 4
    yt = same * y + (1 - same) * yo

    def dev(xx, yy, zz, cc):
        return {"ctx": yy * 4 + zz, "kvh": xx * 2 + cc}

    zr, zl, zf = (z + 1) % 4, (z + 3) % 4, (z + 2) % 4
    xr, xl = (x + 1) % 4, (x + 3) % 4
    SIB = dev(x, y, z, 1 - c)
    PART = dev(x, yp, z, c)
    OPP = dev(x, yo, z, c)
    OPPD = dev(x, yo, z, 1 - c)
    ZR, ZL = dev(x, y, zr, c), dev(x, y, zl, c)
    XR, XL = dev(xr, y, z, c), dev(xl, y, z, c)

    barrier = pltpu.get_barrier_semaphore()
    for t in (SIB, PART, OPP, OPPD, ZR, ZL, XR, XL):
        pl.semaphore_signal(barrier, inc=1, device_id=t, device_id_type=MESH)
    pl.semaphore_wait(barrier, 8)

    def remote(src, dst, ss, rs, target):
        return pltpu.make_async_remote_copy(
            src_ref=src, dst_ref=dst, send_sem=ss, recv_sem=rs,
            device_id=target, device_id_type=MESH,
        )

    bufs = (kv_b, g_b, u_b, d_b)
    ins = (None, g_in, u_in, d_in)
    groups = (z, zl, zr, zf)
    own = 4 * z + y
    extra = (16 + z, 16, 16 + z, 16)
    yb = (y, yp, yo, yq)
    P0 = 2 * h
    P1 = 2 - 2 * h
    sent = {}

    def copy_of(a, idx, half=0):
        def cp(s, d, target, count=1):
            if count == 1:
                src, dst = bufs[a].at[s, c], bufs[a].at[d, c]
            else:
                src = bufs[a].at[pl.ds(s, count), c]
                dst = bufs[a].at[pl.ds(d, count), c]
            return remote(src, dst, send_sem.at[a, idx], recv_sem.at[a, idx], target)

        if idx == 0:
            slot = same * own + (1 - same) * extra[a]
            src = (v_in, k_in)[half] if a == KV else ins[a].at[1 - c]
            return remote(
                src, bufs[a].at[slot, 1 - c], send_sem.at[a, 0], recv_sem.at[a, 0], SIB
            )
        if idx in (17, 18) and a not in (KV, UP):
            s = 4 * zf + (P0 if idx == 17 else P1)
            return cp(s, s, SIB, 2)
        if 14 <= idx < 18:
            s = 4 * groups[idx - 14]
            return cp(s, s, SIB, 4)
        if a in (KV, UP):
            if idx in (4, 6):
                return cp(own, own, ZR if idx == 4 else ZL)
            if idx in (5, 7):
                return cp(16 + z, 16 + z, ZR if idx == 5 else ZL)
            if idx == 8:
                return cp(4 * zl + y, 4 * zl + y, ZR)
            if idx == 9:
                return cp(16 + zr, 16 + zr, ZL)
            zs = groups[idx % 4]
            if 20 <= idx < 24:
                return cp(4 * zs + y, 4 * zs + y, PART)
            if 24 <= idx < 28:
                return cp(16 + zs, 4 * zs + y, OPP)
            return cp(4 * zs + yo, 4 * zs + yo, PART)
        if idx == 1:
            return cp(own, own, PART)
        if idx == 2:
            return cp(16, own, OPP)
        if idx == 3:
            return cp(4 * z + yo, 4 * z + yo, PART)
        if 4 <= idx < 12:
            s = 4 * z + yb[idx % 4]
            return cp(s, s, ZR if idx < 8 else ZL)
        if idx == 12:
            return cp(4 * zl + P0, 4 * zl + P0, ZR, 2)
        return cp(4 * zr + P1, 4 * zr + P1, ZL, 2)

    def local_of(a, half=0):
        slot = same * own + (1 - same) * extra[a]
        src = (k_in, v_in)[half] if a == KV else ins[a].at[c]
        return pltpu.make_async_copy(src, bufs[a].at[slot, c], loc_sem.at[a])

    def go(a, *idxs):
        for idx in idxs:
            copy_of(a, idx).start()
            sent[a, idx] = True

    def got(a, *idxs):
        for idx in idxs:
            copy_of(a, idx).wait_recv()

    def ev_z(a, n):
        if n == 0:
            local_of(a).wait()
            got(a, 0)
            go(a, 1, 2, 4, 8)
        elif n == 1:
            got(a, 1)
            go(a, 5, 9)
        elif n == 2:
            got(a, 2)
            go(a, 3, 6, 10)
        elif n == 3:
            got(a, 3)
            go(a, 7, 11, 14)
        elif n == 4:
            got(a, 4, 5)
            go(a, 12)
        elif n == 5:
            got(a, 10, 11)
            go(a, 13)
        elif n == 6:
            got(a, 6, 7)
            go(a, 15)
            got(a, 8, 9)
            go(a, 16)
        elif n == 7:
            got(a, 12)
            go(a, 17)
            got(a, 13)
            go(a, 18)

    def ev_y(a, n):
        if n == 0:
            local_of(a).wait()
            got(a, 0)
            go(a, 4, 7, 5, 6, 20, 24)
        elif n == 1:
            got(a, 4, 5)
            go(a, 8, 21, 25)
        elif n == 2:
            got(a, 6, 7)
            go(a, 9, 22, 26)
        elif n == 3:
            got(a, 8, 9)
            go(a, 23, 27)
        elif n < 8:
            got(a, 20 + n)
            go(a, 24 + n)
        else:
            got(a, 12 + n, 20 + n)
            go(a, 6 + n)

    k0 = 2 * x + c
    two = pl.ds(2 * x, 2)

    def out_copy(g):
        return remote(o_b.at[g], orx_b.at[g], xs_sem.at[42 + g], xr_sem.at[42 + g], OPPD)

    def xc(i):
        def cp(src, dst, target):
            return remote(src, dst, xs_sem.at[i], xr_sem.at[i], target)

        if i == 0:
            return cp(f_in, f_b.at[k0], SIB)
        if i in (1, 2):
            return remote(
                f_in, f_b.at[k0], xs_sem.at[1], xr_sem.at[1 + c], OPP if i == 1 else OPPD
            )
        if i == 3:
            return cp(q_in, q_b, OPPD)
        if i in (4, 5):
            return cp(f_b.at[two], f_b.at[two], XR if i == 4 else XL)
        if i == 6:
            return cp(f_b.at[2 * xl], f_b.at[2 * xl], XR)
        if i == 7:
            return cp(f_b.at[2 * xr + 1], f_b.at[2 * xr + 1], XL)
        if i == 9:
            return cp(lg_b, lrx_b, OPPD)
        if i < 14:
            n = i - 10
            return cp(r_b.at[n], rx_b.at[n], {"ctx": yo * 4 + z, "kvh": 2 * x + groups[n] // 2})
        if i < 18:
            return cp(r_b.at[i - 14], fo_b.at[i - 14], SIB)
        g, n = (i - 18) // 6, (i - 18) % 6
        lo, hi = pl.ds(0, 256), pl.ds(256, 256)
        if n == 0:
            return cp(ps_b.at[g, 2, lo], fr_b.at[g, 0], XR)
        if n == 1:
            return cp(ps_b.at[g, 2, hi], fr_b.at[g, 1], XL)
        if n == 2:
            return cp(ps_b.at[g, 0, hi], rs_b.at[g, 0, hi], XR)
        if n == 3:
            return cp(ps_b.at[g, 1, lo], rs_b.at[g, 1, lo], XL)
        if n == 4:
            return cp(ps_b.at[g, 0, lo], rs_b.at[g, 0, lo], XR)
        return cp(ps_b.at[g, 1, hi], rs_b.at[g, 1, hi], XL)

    f_loc = pltpu.make_async_copy(f_in, f_b.at[k0], loc_sem.at[4])
    q_loc = pltpu.make_async_copy(q_in, q_b, loc_sem.at[5])

    def start():
        @pl.when(is_same)
        def _():
            f_loc.start()
            q_loc.start()

        @pl.when(not_same)
        def _():
            xc(0).start()
            xc(3).start()

        for half in range(2):
            @pl.when(c == half)
            def _():
                local_of(KV, half).start()
                copy_of(KV, 0, half).start()

        sent[KV, 0] = True
        for a in (GATE, UP, DOWN):
            local_of(a).start()
            go(a, 0)

    def feat(nm):
        if nm == "Fs":
            pl.when(is_same)(lambda: xc(1).start())
            pl.when(not_same)(lambda: xc(2).start())
            return
        n = nm[1]
        if n == "3":
            xc(6).wait_recv()
            xc(7).wait_recv()
            return

        @pl.when(is_same if nm[2] == "a" else not_same)
        def _():
            if nm == "F0a":
                f_loc.wait()
                xc(0).wait_recv()
            elif nm == "F0b":
                for j in range(2):
                    remote(f_in, f_b.at[0], xs_sem.at[1], xr_sem.at[1 + j], OPP).wait_recv()
            if n == "0":
                xc(4).start()
                xc(5).start()
            elif n == "1":
                xc(4).wait_recv()
                xc(6).start()
            else:
                xc(5).wait_recv()
                xc(7).start()

    def q_wait():
        pl.when(is_same)(lambda: q_loc.wait())
        pl.when(not_same)(lambda: xc(3).wait())

    my_span = span_ref[yt * 4 + z]

    step = 128

    def tile(g, t, q, k, va, hide, first):
        rows = slice(t * step, t * step + step)
        s = lax.dot_general(q, k, (((1,), (1,)), ((), ())), preferred_element_type=F32)
        if first:
            ri = lax.broadcasted_iota(jnp.int32, (step, TOK), 0) + t * step
            ci = lax.broadcasted_iota(jnp.int32, (step, TOK), 1)
            s = jnp.where(ci <= ri, s, -1e30)
            m_new = jnp.broadcast_to(jnp.max(s, axis=1, keepdims=True), (step, HD)) * SCALE2
            p = jnp.exp2(s * SCALE2 - jnp.concatenate([m_new] * 4, axis=1))
            acc_b[g, rows] = jnp.dot(p.astype(BF), va, preferred_element_type=F32)
        else:
            m_old = m_b[g, rows]
            top = jnp.max(s, axis=1, keepdims=True) * SCALE2 - hide
            m_new = jnp.maximum(m_old, top)
            alpha = jnp.exp2(m_old - m_new)
            sub = m_new + hide
            p = jnp.exp2(s * SCALE2 - jnp.concatenate([sub] * 4, axis=1))
            pv = jnp.dot(p.astype(BF), va, preferred_element_type=F32)
            acc_b[g, rows] = acc_b[g, rows] * jnp.concatenate([alpha] * 2, axis=1) + pv
        m_b[g, rows] = m_new

    def operands(slot, src):
        hide = jnp.where(span_ref[src] < my_span, 0.0, 1e30).astype(F32)
        k = kv_b[slot, 0]
        return hide, k, jnp.concatenate([kv_b[slot, 1], jnp.ones((TOK, HD), BF)], axis=1)

    def attend(slot, src, first):
        hide, k, va = operands(slot, src)
        for g in range(4):
            for t in range(TOK // step):
                q = q_b[t * step : t * step + step, g * HD : g * HD + HD]
                tile(g, t, q, k, va, hide, first)

    def attend_head(g):
        col = pl.ds(pl.multiple_of(g * HD, HD), HD)
        for ys in range(4):
            hide, k, va = operands(4 * zf + ys, 4 * ys + zf)
            for t in range(TOK // step):
                tile(g, t, q_b[t * step : t * step + step, col], k, va, hide, False)
        total = acc_b[g, :, HD:]
        o_b[g] = (acc_b[g, :, :HD] / total).astype(BF)
        logs = m_b[g] * (1.0 / LOG2E) + jnp.log(total)
        lg_b[g] = jnp.transpose(logs)[:8]

        @pl.when(not_same)
        def _():
            out_copy(g).start()

    def finish():
        @pl.when(is_same)
        def _():
            for g in range(4):
                att_out[:, g * HD : g * HD + HD] = o_b[g]
                log_out[pl.ds(g, 1)] = lg_b[g, :1]

        @pl.when(not_same)
        def _():
            xc(9).start()

    def norm():
        gains = [gain_ref[k * TOK : (k + 1) * TOK].reshape(1, TOK) for k in range(8)]

        def rows_of(i, _):
            rows = pl.ds(i * 64, 64)
            part = jnp.zeros((64, TOK), F32)
            for k in range(8):
                v = f_b[k, rows].astype(F32)
                part = part + v * v
            r = lax.rsqrt(jnp.sum(part, axis=1, keepdims=True) * (1.0 / 4096) + 1e-05)
            for k in range(8):
                n_b[k, rows] = (f_b[k, rows].astype(F32) * r * gains[k]).astype(BF)
            return 0

        lax.fori_loop(0, 8, rows_of, 0)

    def project(a, i):
        zs = groups[i]
        out = ga_b if a == GATE else ua_b
        off = pl.multiple_of((zs % 2) * 256, 256)

        def rows_of(t, _):
            rows = pl.ds(t * 256, 256)
            lhs = jnp.concatenate(
                [n_b[2 * ys + zs // 2, rows, pl.ds(off, 256)] for ys in range(4)], axis=1
            )
            w = bufs[a][pl.ds(4 * zs, 4)].reshape(1024, 896)
            res = jnp.dot(lhs, w, preferred_element_type=F32)
            if i == 0:
                out[rows] = res
            else:
                out[rows] = out[rows] + res
            return 0

        lax.fori_loop(0, 2, rows_of, 0)

    def act():
        def rows_of(i, _):
            rows = pl.ds(i * 64, 64)
            g = ga_b[rows]
            hid_b[rows] = (g / (1.0 + jnp.exp(-g)) * ua_b[rows]).astype(BF)
            return 0

        lax.fori_loop(0, 8, rows_of, 0)

    def x_go(i, *ns):
        for n in ns:
            xc(18 + 6 * i + n).start()
            sent[18 + 6 * i + n] = True

    def x_got(i, *ns):
        for n in ns:
            xc(18 + 6 * i + n).wait_recv()

    def down(i, n):
        xd = (xr, xl, (x + 2) % 4, x)[n]
        w = d_b[4 * groups[i] + xd].reshape(896, 256)
        res = jnp.dot(hid_b[...], w, preferred_element_type=F32)
        if n == 3:
            po_b[i] = res
            return
        ps_b[i, n] = res.astype(BF)
        if n == 2:
            x_go(i, 0, 1)
        else:
            x_go(i, 2 + n)

    def forward(i, n):
        x_got(i, n)
        rows = pl.ds(256 * n, 256)
        ps_b[i, n, rows] = (ps_b[i, n, rows].astype(F32) + fr_b[i, n].astype(F32)).astype(BF)
        x_go(i, 4 + n)

    def combine(i):
        x_got(i, 2, 3, 4, 5)
        total = po_b[i] + rs_b[i, 0].astype(F32) + rs_b[i, 1].astype(F32)
        r_b[i] = total.astype(BF)

        @pl.when(not_same)
        def _():
            xc(10 + i).start()

        @pl.when(is_same & (groups[i] // 2 != c))
        def _():
            xc(14 + i).start()

    def close(i):
        zs = groups[i]
        off = pl.multiple_of((zs % 2) * 256, 256)

        @pl.when(zs // 2 == c)
        def _():
            xc(10 + i).wait_recv()

            @pl.when(is_same)
            def _():
                res = r_b[i].astype(F32) + rx_b[i].astype(F32)
                ffn_out[:, pl.ds(off, 256)] = res.astype(BF)

            @pl.when(not_same)
            def _():
                xc(14 + i).wait_recv()
                res = fo_b[i].astype(F32) + rx_b[i].astype(F32)
                ffn_out[:, pl.ds(off, 256)] = res.astype(BF)

    def run(nm):
        if nm == "st":
            start()
        elif nm[0] == "F":
            feat(nm)
        elif nm == "Q":
            q_wait()
        elif nm == "AF":
            finish()
        elif nm == "N":
            norm()
        elif nm == "ACT":
            act()
        elif nm[0] == "P":
            project("KGUD".index(nm[1]), int(nm[2]))
        elif nm[0] == "W":
            down(int(nm[1]), int(nm[2]))
        elif nm[0] == "X":
            forward(int(nm[1]), int(nm[2]))
        elif nm[0] == "C":
            combine(int(nm[1]))
        elif nm[0] == "E":
            close(int(nm[1]))
        else:
            a = "KGUD".index(nm[0])
            if nm[1] == "r":
                got(a, 14 + int(nm[2]))
                if nm[2] == "3" and a not in (KV, UP):
                    got(a, 18)
            elif a in (KV, UP):
                ev_y(a, int(nm[1:]))
            else:
                ev_z(a, int(nm[1:]))

    parts = [[]]
    for nm in ORDER:
        if nm[0] == "A" and nm[1:].isdigit():
            parts.append([])
        else:
            parts[-1].append(nm)
    for nm in parts[0]:
        run(nm)
    attend(4 * z + yt, yt * 4 + z, True)
    for nm in parts[1]:
        run(nm)

    def block(n, _):
        i, j = n // 4, n % 4
        delta = (i // 2) * (i - 1) + (1 - i // 2) * (3 * i)
        zs = (z + delta) % 4
        ys = (yt + j) % 4
        attend(4 * zs + ys, ys * 4 + zs, False)
        for m in range(1, 12):
            if parts[m + 1]:
                @pl.when(n == m)
                def _():
                    for nm in parts[m + 1]:
                        run(nm)
        return 0

    lax.fori_loop(1, 12, block, 0)

    def last(g, _):
        attend_head(g)
        for m in range(3):
            if parts[13 + m]:
                @pl.when(g == m)
                def _():
                    for nm in parts[13 + m]:
                        run(nm)
        return 0

    lax.fori_loop(0, 4, last, 0)
    for nm in parts[16]:
        run(nm)

    @pl.when(is_same)
    def _():
        xc(1).wait_send()
        for i in range(4):
            pl.when(groups[i] // 2 != c)(lambda: xc(14 + i).wait_send())

    @pl.when(not_same)
    def _():
        xc(0).wait_send()
        xc(2).wait_send()
        xc(9).wait()
        for g in range(4):
            log_out[pl.ds(g, 1)] = lrx_b[g, :1]
            out_copy(g).wait()
            att_out[:, g * HD : g * HD + HD] = orx_b[g]
        for i in range(4):
            xc(10 + i).wait_send()

    for i in (4, 5, 6, 7):
        xc(i).wait_send()
    for it in sent:
        if isinstance(it, tuple):
            copy_of(*it).wait_send()
        else:
            xc(it).wait_send()


def body(queries, keys, values, span_order, ffn_input, norm_gain, gate_w, up_w, down_w):
    anyspace = pl.BlockSpec(memory_space=pl.ANY)
    vmem = pl.BlockSpec(memory_space=pltpu.VMEM)
    smem = pl.BlockSpec(memory_space=pltpu.SMEM)
    sem = pltpu.SemaphoreType.DMA
    return pl.pallas_call(
        kernel,
        out_shape=(
            jax.ShapeDtypeStruct((512, 512), BF),
            jax.ShapeDtypeStruct((4, 512), F32),
            jax.ShapeDtypeStruct((512, 512), BF),
        ),
        in_specs=[smem, vmem] + [anyspace] * 7,
        out_specs=(vmem, vmem, vmem),
        scratch_shapes=[
            pltpu.VMEM((20, 2, 512, 128), BF),
            pltpu.VMEM((17, 2, 128, 896), BF),
            pltpu.VMEM((20, 2, 128, 896), BF),
            pltpu.VMEM((17, 2, 448, 256), BF),
            pltpu.VMEM((512, 512), BF),
            pltpu.VMEM((8, 512, 512), BF),
            pltpu.VMEM((8, 512, 512), BF),
            pltpu.VMEM((4, 512, 128), F32),
            pltpu.VMEM((4, 512, 256), F32),
            pltpu.VMEM((4, 512, 128), BF),
            pltpu.VMEM((4, 512, 128), BF),
            pltpu.VMEM((4, 8, 512), F32),
            pltpu.VMEM((4, 8, 512), F32),
            pltpu.VMEM((512, 896), F32),
            pltpu.VMEM((512, 896), F32),
            pltpu.VMEM((512, 896), BF),
            pltpu.VMEM((4, 3, 512, 256), BF),
            pltpu.VMEM((4, 512, 256), F32),
            pltpu.VMEM((4, 2, 256, 256), BF),
            pltpu.VMEM((4, 2, 512, 256), BF),
            pltpu.VMEM((4, 512, 256), BF),
            pltpu.VMEM((4, 512, 256), BF),
            pltpu.VMEM((4, 512, 256), BF),
            sem((6,)),
            sem((4, 32)),
            sem((4, 32)),
            sem((46,)),
            sem((46,)),
        ],
        compiler_params=pltpu.CompilerParams(
            collective_id=0, has_side_effects=True, vmem_limit_bytes=63 * 2**20
        ),
        name="layer",
    )(
        span_order,
        norm_gain,
        queries,
        keys,
        values,
        ffn_input,
        gate_w.reshape(2, 128, 896),
        up_w.reshape(2, 128, 896),
        down_w.reshape(2, 448, 256),
    )


def solution(mesh):
    placed = (
        P("ctx", "kvh"), P("ctx", "kvh"), P("ctx", "kvh"), P(), P("ctx", "kvh"), P(),
        P("ctx", "kvh"), P("ctx", "kvh"), P("kvh", "ctx"),
    )
    return jax.shard_map(
        body,
        mesh=mesh,
        in_specs=placed,
        out_specs=(P("ctx", "kvh"), P("kvh", "ctx"), P("ctx", "kvh")),
        check_vma=False,
    )
```

```python
import functools
import math

import jax
import jax.numpy as jnp
from jax import lax
from jax.experimental import pallas as pl
from jax.experimental.pallas import tpu as pltpu
from jax.sharding import PartitionSpec as P

MESH = pl.DeviceIdType.MESH
HD = 128
TOK = 512
BF = jnp.bfloat16
F32 = jnp.float32
KV, GATE, UP, DOWN = range(4)
LOG2E = math.log2(math.e)
SCALE2 = LOG2E / math.sqrt(HD)

ORDER = (
    "st", "K0", "K12", "U0", "U12", "G0", "Fs", "F0a", "K4", "G2", "K1", "F1a", "U1", "U13", "U2",
    "F2a", "G1", "U14", "U4", "K2", "F0b", "Qs", "U5", "G3", "K8", "Kr0", "U8", "U3", "U6", "D0",
    "Ur0", "F1b", "F2b", "Q", "G4", "U15", "A00", "G5", "G6", "U9", "A01", "A02", "F3", "G8", "K3",
    "N", "A03", "Gr1", "U7", "U10", "D2", "K13", "Gr0", "PG0", "PG1", "PU0", "Ur2", "K5", "D1",
    "G7", "K15", "PU2", "Gr2", "K14", "U11", "Ur1", "PG2", "PU1", "Gr3", "PG3", "D3", "Ur3", "PU3",
    "ACT", "Dr0", "W02", "W00", "D4", "W03", "K9", "K6", "W01", "D6", "D5", "K7", "D8", "X01",
    "X00", "Kr1", "A10", "A11", "Dr1", "W12", "W10", "A12", "K10", "Dr2", "W11", "W22", "A13",
    "X10", "W20", "Kr2", "D7", "K11", "A20", "X11", "A21", "W13", "Dr3", "W21", "X21", "X20", "W23",
    "Kr3", "W32", "C0", "C1", "W31", "A22", "A23", "A30", "W30", "C2", "A31", "X30", "X31", "A32",
    "A33", "AF", "E0", "W33", "C3", "E1", "E2", "E3",
)


def kernel(
    span_ref, gain_ref, q_in, k_in, v_in, f_in, g_in, u_in, d_in,
    att_out, log_out, ffn_out,
    kv_b, g_b, u_b, d_b,
    q_b, f_b, n_b, m_b, acc_b, o_b, orx_b, lg_b, lrx_b,
    ga_b, ua_b, hid_b, ps_b, po_b, fr_b, rs_b, r_b, rx_b, fo_b,
    loc_sem, send_sem, recv_sem, xs_sem, xr_sem,
):
    ctx = lax.axis_index("ctx")
    kvh = lax.axis_index("kvh")
    x, c = kvh // 2, kvh % 2
    y, z = ctx // 4, ctx % 4
    h = y // 2
    same = c * h + (1 - c) * (1 - h)
    is_same = c == h
    not_same = c != h
    yp = y + 1 - 2 * (y % 2)
    yo = 3 - y
    yq = (y + 2) % 4
    yt = same * y + (1 - same) * yo

    def dev(xx, yy, zz, cc):
        return {"ctx": yy * 4 + zz, "kvh": xx * 2 + cc}

    zr, zl, zf = (z + 1) % 4, (z + 3) % 4, (z + 2) % 4
    xr, xl = (x + 1) % 4, (x + 3) % 4
    SIB = dev(x, y, z, 1 - c)
    PART = dev(x, yp, z, c)
    OPP = dev(x, yo, z, c)
    OPPD = dev(x, yo, z, 1 - c)
    ZR, ZL = dev(x, y, zr, c), dev(x, y, zl, c)
    XR, XL = dev(xr, y, z, c), dev(xl, y, z, c)

    barrier = pltpu.get_barrier_semaphore()
    for t in (SIB, PART, OPP, OPPD, ZR, ZL, XR, XL):
        pl.semaphore_signal(barrier, inc=1, device_id=t, device_id_type=MESH)
    pl.semaphore_wait(barrier, 8)

    def remote(src, dst, ss, rs, target):
        return pltpu.make_async_remote_copy(
            src_ref=src, dst_ref=dst, send_sem=ss, recv_sem=rs,
            device_id=target, device_id_type=MESH,
        )

    bufs = (kv_b, g_b, u_b, d_b)
    ins = (None, g_in, u_in, d_in)
    groups = (z, zl, zr, zf)
    own = 4 * z + y
    extra = (16 + z, 16, 16 + z, 16)
    yb = (y, yp, yo, yq)
    P0 = 2 * h
    P1 = 2 - 2 * h
    sent = {}

    def copy_of(a, idx, half=0):
        def cp(s, d, target, count=1):
            if count == 1:
                src, dst = bufs[a].at[s, c], bufs[a].at[d, c]
            else:
                src = bufs[a].at[pl.ds(s, count), c]
                dst = bufs[a].at[pl.ds(d, count), c]
            return remote(src, dst, send_sem.at[a, idx], recv_sem.at[a, idx], target)

        if idx == 0:
            slot = same * own + (1 - same) * extra[a]
            src = (v_in, k_in)[half] if a == KV else ins[a].at[1 - c]
            return remote(
                src, bufs[a].at[slot, 1 - c], send_sem.at[a, 0], recv_sem.at[a, 0], SIB
            )
        if idx in (17, 18) and a not in (KV, UP):
            s = 4 * zf + (P0 if idx == 17 else P1)
            return cp(s, s, SIB, 2)
        if 14 <= idx < 18:
            s = 4 * groups[idx - 14]
            return cp(s, s, SIB, 4)
        if a in (KV, UP):
            if idx in (4, 6):
                return cp(own, own, ZR if idx == 4 else ZL)
            if idx in (5, 7):
                return cp(16 + z, 16 + z, ZR if idx == 5 else ZL)
            if idx == 8:
                return cp(4 * zl + y, 4 * zl + y, ZR)
            if idx == 9:
                return cp(16 + zr, 16 + zr, ZL)
            zs = groups[idx % 4]
            if 20 <= idx < 24:
                return cp(4 * zs + y, 4 * zs + y, PART)
            if 24 <= idx < 28:
                return cp(16 + zs, 4 * zs + y, OPP)
            return cp(4 * zs + yo, 4 * zs + yo, PART)
        if idx == 1:
            return cp(own, own, PART)
        if idx == 2:
            return cp(16, own, OPP)
        if idx == 3:
            return cp(4 * z + yo, 4 * z + yo, PART)
        if 4 <= idx < 12:
            s = 4 * z + yb[idx % 4]
            return cp(s, s, ZR if idx < 8 else ZL)
        if idx == 12:
            return cp(4 * zl + P0, 4 * zl + P0, ZR, 2)
        return cp(4 * zr + P1, 4 * zr + P1, ZL, 2)

    def local_of(a, half=0):
        slot = same * own + (1 - same) * extra[a]
        src = (k_in, v_in)[half] if a == KV else ins[a].at[c]
        return pltpu.make_async_copy(src, bufs[a].at[slot, c], loc_sem.at[a])

    def go(a, *idxs):
        for idx in idxs:
            copy_of(a, idx).start()
            sent[a, idx] = True

    def got(a, *idxs):
        for idx in idxs:
            copy_of(a, idx).wait_recv()

    def first(a, mine, other):
        local_of(a).wait()
        pl.when(is_same)(lambda: go(a, *mine))
        pl.when(not_same)(lambda: go(a, *other))
        got(a, 0)
        pl.when(is_same)(lambda: go(a, *other))
        pl.when(not_same)(lambda: go(a, *mine))

    def ev_z(a, n):
        if n == 0:
            first(a, (1, 4, 8), (2,))
        elif n == 1:
            got(a, 1)
            go(a, 5, 9)
        elif n == 2:
            got(a, 2)
            go(a, 3, 6, 10)
        elif n == 3:
            got(a, 3)
            go(a, 7, 11, 14)
        elif n == 4:
            got(a, 4, 5)
            go(a, 12)
        elif n == 5:
            got(a, 10, 11)
            go(a, 13)
        elif n == 6:
            got(a, 6, 7)
            go(a, 15)
        elif n == 8:
            got(a, 8, 9)
            go(a, 16)
        elif n == 7:
            got(a, 12)
            go(a, 17)
            got(a, 13)
            go(a, 18)

    def ev_y(a, n):
        if n == 0:
            first(a, (4, 6), (5, 7))
        elif n == 1:
            got(a, 4, 5)
            go(a, 8)
        elif n == 2:
            got(a, 6, 7)
            go(a, 9)
        elif n == 3:
            got(a, 8, 9)
        elif n < 8:
            got(a, 20 + n)
            go(a, 24 + n)
        elif n >= 12:
            go(a, 8 + n, 12 + n)
        else:
            got(a, 12 + n, 20 + n)
            go(a, 6 + n)

    k0 = 2 * x + c
    two = pl.ds(2 * x, 2)

    def out_copy(g):
        return remote(o_b.at[g], orx_b.at[g], xs_sem.at[42 + g], xr_sem.at[42 + g], OPPD)

    def xc(i):
        def cp(src, dst, target):
            return remote(src, dst, xs_sem.at[i], xr_sem.at[i], target)

        if i == 0:
            return cp(f_in, f_b.at[k0], SIB)
        if i in (1, 2):
            return remote(
                f_in, f_b.at[k0], xs_sem.at[1], xr_sem.at[1 + c], OPP if i == 1 else OPPD
            )
        if i == 3:
            return cp(q_in, q_b, OPPD)
        if i in (4, 5):
            return cp(f_b.at[two], f_b.at[two], XR if i == 4 else XL)
        if i == 6:
            return cp(f_b.at[2 * xl], f_b.at[2 * xl], XR)
        if i == 7:
            return cp(f_b.at[2 * xr + 1], f_b.at[2 * xr + 1], XL)
        if i == 9:
            return cp(lg_b, lrx_b, OPPD)
        if i < 14:
            n = i - 10
            return cp(r_b.at[n], rx_b.at[n], {"ctx": yo * 4 + z, "kvh": 2 * x + groups[n] // 2})
        if i < 18:
            return cp(r_b.at[i - 14], fo_b.at[i - 14], SIB)
        g, n = (i - 18) // 6, (i - 18) % 6
        lo, hi = pl.ds(0, 256), pl.ds(256, 256)
        if n == 0:
            return cp(ps_b.at[g, 2, lo], fr_b.at[g, 0], XR)
        if n == 1:
            return cp(ps_b.at[g, 2, hi], fr_b.at[g, 1], XL)
        if n == 2:
            return cp(ps_b.at[g, 0, hi], rs_b.at[g, 0, hi], XR)
        if n == 3:
            return cp(ps_b.at[g, 1, lo], rs_b.at[g, 1, lo], XL)
        if n == 4:
            return cp(ps_b.at[g, 0, lo], rs_b.at[g, 0, lo], XR)
        return cp(ps_b.at[g, 1, hi], rs_b.at[g, 1, hi], XL)

    f_loc = pltpu.make_async_copy(f_in, f_b.at[k0], loc_sem.at[4])
    q_loc = pltpu.make_async_copy(q_in, q_b, loc_sem.at[5])

    def start():
        @pl.when(is_same)
        def _():
            f_loc.start()

        @pl.when(not_same)
        def _():
            xc(0).start()

        for half in range(2):
            @pl.when(c == half)
            def _():
                local_of(KV, half).start()
                copy_of(KV, 0, half).start()

        sent[KV, 0] = True
        for a in (GATE, UP, DOWN):
            local_of(a).start()
            go(a, 0)

    def feat(nm):
        if nm == "Fs":
            pl.when(is_same)(lambda: xc(1).start())
            pl.when(not_same)(lambda: xc(2).start())
            return
        n = nm[1]
        if n == "3":
            xc(6).wait_recv()
            xc(7).wait_recv()
            return

        @pl.when(is_same if nm[2] == "a" else not_same)
        def _():
            if nm == "F0a":
                f_loc.wait()
                xc(0).wait_recv()
            elif nm == "F0b":
                for j in range(2):
                    remote(f_in, f_b.at[0], xs_sem.at[1], xr_sem.at[1 + j], OPP).wait_recv()
            if n == "0":
                xc(4).start()
                xc(5).start()
            elif n == "1":
                xc(4).wait_recv()
                xc(6).start()
            else:
                xc(5).wait_recv()
                xc(7).start()

    def q_wait():
        pl.when(is_same)(lambda: q_loc.wait())
        pl.when(not_same)(lambda: xc(3).wait())

    my_span = span_ref[yt * 4 + z]

    step = 128

    def tile(g, t, q, k, va, hide, first):
        rows = slice(t * step, t * step + step)
        s = lax.dot_general(q, k, (((1,), (1,)), ((), ())), preferred_element_type=F32)
        if first:
            ri = lax.broadcasted_iota(jnp.int32, (step, TOK), 0) + t * step
            ci = lax.broadcasted_iota(jnp.int32, (step, TOK), 1)
            s = jnp.where(ci <= ri, s, -1e30)
            m_new = jnp.broadcast_to(jnp.max(s, axis=1, keepdims=True), (step, HD)) * SCALE2
            p = jnp.exp2(s * SCALE2 - jnp.concatenate([m_new] * 4, axis=1))
            acc_b[g, rows] = jnp.dot(p.astype(BF), va, preferred_element_type=F32)
        else:
            m_old = m_b[g, rows]
            top = jnp.max(s, axis=1, keepdims=True) * SCALE2 - hide
            m_new = jnp.maximum(m_old, top)
            alpha = jnp.exp2(m_old - m_new)
            sub = m_new + hide
            p = jnp.exp2(s * SCALE2 - jnp.concatenate([sub] * 4, axis=1))
            pv = jnp.dot(p.astype(BF), va, preferred_element_type=F32)
            acc_b[g, rows] = acc_b[g, rows] * jnp.concatenate([alpha] * 2, axis=1) + pv
        m_b[g, rows] = m_new

    def operands(slot, src):
        hide = jnp.where(span_ref[src] < my_span, 0.0, 1e30).astype(F32)
        k = kv_b[slot, 0]
        return hide, k, jnp.concatenate([kv_b[slot, 1], jnp.ones((TOK, HD), BF)], axis=1)

    def attend(slot, src, first):
        hide, k, va = operands(slot, src)
        for g in range(4):
            for t in range(TOK // step):
                q = q_b[t * step : t * step + step, g * HD : g * HD + HD]
                tile(g, t, q, k, va, hide, first)

    def attend_head(g):
        col = pl.ds(pl.multiple_of(g * HD, HD), HD)
        for ys in range(4):
            hide, k, va = operands(4 * zf + ys, 4 * ys + zf)
            for t in range(TOK // step):
                tile(g, t, q_b[t * step : t * step + step, col], k, va, hide, False)
        total = acc_b[g, :, HD:]
        o_b[g] = (acc_b[g, :, :HD] / total).astype(BF)
        logs = m_b[g] * (1.0 / LOG2E) + jnp.log(total)
        lg_b[g] = jnp.transpose(logs)[:8]

        @pl.when(not_same)
        def _():
            out_copy(g).start()

    def finish():
        @pl.when(is_same)
        def _():
            for g in range(4):
                att_out[:, g * HD : g * HD + HD] = o_b[g]
                log_out[pl.ds(g, 1)] = lg_b[g, :1]

        @pl.when(not_same)
        def _():
            xc(9).start()

    def norm():
        gains = [gain_ref[k * TOK : (k + 1) * TOK].reshape(1, TOK) for k in range(8)]

        def rows_of(i, _):
            rows = pl.ds(i * 64, 64)
            part = jnp.zeros((64, TOK), F32)
            for k in range(8):
                v = f_b[k, rows].astype(F32)
                part = part + v * v
            r = lax.rsqrt(jnp.sum(part, axis=1, keepdims=True) * (1.0 / 4096) + 1e-05)
            for k in range(8):
                n_b[k, rows] = (f_b[k, rows].astype(F32) * r * gains[k]).astype(BF)
            return 0

        lax.fori_loop(0, 8, rows_of, 0)

    def project(a, i):
        zs = groups[i]
        out = ga_b if a == GATE else ua_b
        off = pl.multiple_of((zs % 2) * 256, 256)

        def rows_of(t, _):
            rows = pl.ds(t * 256, 256)
            lhs = jnp.concatenate(
                [n_b[2 * ys + zs // 2, rows, pl.ds(off, 256)] for ys in range(4)], axis=1
            )
            w = bufs[a][pl.ds(4 * zs, 4)].reshape(1024, 896)
            res = jnp.dot(lhs, w, preferred_element_type=F32)
            if i == 0:
                out[rows] = res
            else:
                out[rows] = out[rows] + res
            return 0

        lax.fori_loop(0, 2, rows_of, 0)

    def act():
        def rows_of(i, _):
            rows = pl.ds(i * 64, 64)
            g = ga_b[rows]
            hid_b[rows] = (g / (1.0 + jnp.exp(-g)) * ua_b[rows]).astype(BF)
            return 0

        lax.fori_loop(0, 8, rows_of, 0)

    def x_go(i, *ns):
        for n in ns:
            xc(18 + 6 * i + n).start()
            sent[18 + 6 * i + n] = True

    def x_got(i, *ns):
        for n in ns:
            xc(18 + 6 * i + n).wait_recv()

    def down(i, n):
        xd = (xr, xl, (x + 2) % 4, x)[n]
        w = d_b[4 * groups[i] + xd].reshape(896, 256)
        res = jnp.dot(hid_b[...], w, preferred_element_type=F32)
        if n == 3:
            po_b[i] = res
            return
        ps_b[i, n] = res.astype(BF)
        if n == 2:
            x_go(i, 0, 1)
        else:
            x_go(i, 2 + n)

    def forward(i, n):
        x_got(i, n)
        rows = pl.ds(256 * n, 256)
        ps_b[i, n, rows] = (ps_b[i, n, rows].astype(F32) + fr_b[i, n].astype(F32)).astype(BF)
        x_go(i, 4 + n)

    def combine(i):
        x_got(i, 2, 3, 4, 5)
        total = po_b[i] + rs_b[i, 0].astype(F32) + rs_b[i, 1].astype(F32)
        r_b[i] = total.astype(BF)

        @pl.when(not_same)
        def _():
            xc(10 + i).start()

        @pl.when(is_same & (groups[i] // 2 != c))
        def _():
            xc(14 + i).start()

    def close(i):
        zs = groups[i]
        off = pl.multiple_of((zs % 2) * 256, 256)

        @pl.when(zs // 2 == c)
        def _():
            xc(10 + i).wait_recv()

            @pl.when(is_same)
            def _():
                res = r_b[i].astype(F32) + rx_b[i].astype(F32)
                ffn_out[:, pl.ds(off, 256)] = res.astype(BF)

            @pl.when(not_same)
            def _():
                xc(14 + i).wait_recv()
                res = fo_b[i].astype(F32) + rx_b[i].astype(F32)
                ffn_out[:, pl.ds(off, 256)] = res.astype(BF)

    def run(nm):
        if nm == "st":
            start()
        elif nm[0] == "F":
            feat(nm)
        elif nm == "Qs":
            pl.when(is_same)(lambda: q_loc.start())
            pl.when(not_same)(lambda: xc(3).start())
        elif nm == "Q":
            q_wait()
        elif nm == "AF":
            finish()
        elif nm == "N":
            norm()
        elif nm == "ACT":
            act()
        elif nm[0] == "P":
            project("KGUD".index(nm[1]), int(nm[2]))
        elif nm[0] == "W":
            down(int(nm[1]), int(nm[2]))
        elif nm[0] == "X":
            forward(int(nm[1]), int(nm[2]))
        elif nm[0] == "C":
            combine(int(nm[1]))
        elif nm[0] == "E":
            close(int(nm[1]))
        else:
            a = "KGUD".index(nm[0])
            if nm[1] == "r":
                got(a, 14 + int(nm[2]))
                if nm[2] == "3" and a not in (KV, UP):
                    got(a, 18)
            elif a in (KV, UP):
                ev_y(a, int(nm[1:]))
            else:
                ev_z(a, int(nm[1:]))

    parts = [[]]
    for nm in ORDER:
        if nm[0] == "A" and nm[1:].isdigit():
            parts.append([])
        else:
            parts[-1].append(nm)
    for nm in parts[0]:
        run(nm)
    attend(4 * z + yt, yt * 4 + z, True)
    for nm in parts[1]:
        run(nm)

    def block(n, _):
        i, j = n // 4, n % 4
        delta = (i // 2) * (i - 1) + (1 - i // 2) * (3 * i)
        zs = (z + delta) % 4
        ys = (yt + j) % 4
        attend(4 * zs + ys, ys * 4 + zs, False)
        for m in range(1, 12):
            if parts[m + 1]:
                @pl.when(n == m)
                def _():
                    for nm in parts[m + 1]:
                        run(nm)
        return 0

    lax.fori_loop(1, 12, block, 0)

    def last(g, _):
        attend_head(g)
        for m in range(3):
            if parts[13 + m]:
                @pl.when(g == m)
                def _():
                    for nm in parts[13 + m]:
                        run(nm)
        return 0

    lax.fori_loop(0, 4, last, 0)
    for nm in parts[16]:
        run(nm)

    @pl.when(is_same)
    def _():
        xc(1).wait_send()
        for i in range(4):
            pl.when(groups[i] // 2 != c)(lambda: xc(14 + i).wait_send())

    @pl.when(not_same)
    def _():
        xc(0).wait_send()
        xc(2).wait_send()
        xc(9).wait()
        for g in range(4):
            log_out[pl.ds(g, 1)] = lrx_b[g, :1]
            out_copy(g).wait()
            att_out[:, g * HD : g * HD + HD] = orx_b[g]
        for i in range(4):
            xc(10 + i).wait_send()

    for i in (4, 5, 6, 7):
        xc(i).wait_send()
    for it in sent:
        if isinstance(it, tuple):
            copy_of(*it).wait_send()
        else:
            xc(it).wait_send()


def move(a_in, l_in, f_in, a_out, l_out, f_out):
    a_out[...] = a_in[...]
    l_out[...] = l_in[...]
    f_out[...] = f_in[...]


def body(queries, keys, values, span_order, ffn_input, norm_gain, gate_w, up_w, down_w):
    anyspace = pl.BlockSpec(memory_space=pl.ANY)
    vmem = pl.BlockSpec(memory_space=pltpu.VMEM)
    smem = pl.BlockSpec(memory_space=pltpu.SMEM)
    sem = pltpu.SemaphoreType.DMA
    shapes = (
        jax.ShapeDtypeStruct((512, 512), BF),
        jax.ShapeDtypeStruct((4, 512), F32),
        jax.ShapeDtypeStruct((512, 512), BF),
    )
    outs = pl.pallas_call(
        kernel,
        out_shape=shapes,
        in_specs=[smem, vmem] + [anyspace] * 7,
        out_specs=(vmem, vmem, vmem),
        scratch_shapes=[
            pltpu.VMEM((20, 2, 512, 128), BF),
            pltpu.VMEM((17, 2, 128, 896), BF),
            pltpu.VMEM((20, 2, 128, 896), BF),
            pltpu.VMEM((17, 2, 448, 256), BF),
            pltpu.VMEM((512, 512), BF),
            pltpu.VMEM((8, 512, 512), BF),
            pltpu.VMEM((8, 512, 512), BF),
            pltpu.VMEM((4, 512, 128), F32),
            pltpu.VMEM((4, 512, 256), F32),
            pltpu.VMEM((4, 512, 128), BF),
            pltpu.VMEM((4, 512, 128), BF),
            pltpu.VMEM((4, 8, 512), F32),
            pltpu.VMEM((4, 8, 512), F32),
            pltpu.VMEM((512, 896), F32),
            pltpu.VMEM((512, 896), F32),
            pltpu.VMEM((512, 896), BF),
            pltpu.VMEM((4, 3, 512, 256), BF),
            pltpu.VMEM((4, 512, 256), F32),
            pltpu.VMEM((4, 2, 256, 256), BF),
            pltpu.VMEM((4, 2, 512, 256), BF),
            pltpu.VMEM((4, 512, 256), BF),
            pltpu.VMEM((4, 512, 256), BF),
            pltpu.VMEM((4, 512, 256), BF),
            sem((6,)),
            sem((4, 32)),
            sem((4, 32)),
            sem((46,)),
            sem((46,)),
        ],
        compiler_params=pltpu.CompilerParams(
            collective_id=0, has_side_effects=True, vmem_limit_bytes=63 * 2**20
        ),
        name="layer",
    )(
        span_order,
        norm_gain,
        queries,
        keys,
        values,
        ffn_input,
        gate_w.reshape(2, 128, 896),
        up_w.reshape(2, 128, 896),
        down_w.reshape(2, 448, 256),
    )
    return pl.pallas_call(
        move,
        out_shape=shapes,
        in_specs=[vmem] * 3,
        out_specs=(vmem,) * 3,
        name="move",
    )(*outs)


def solution(mesh):
    placed = (
        P("ctx", "kvh"), P("ctx", "kvh"), P("ctx", "kvh"), P(), P("ctx", "kvh"), P(),
        P("ctx", "kvh"), P("ctx", "kvh"), P("kvh", "ctx"),
    )
    return jax.shard_map(
        body,
        mesh=mesh,
        in_specs=placed,
        out_specs=(P("ctx", "kvh"), P("kvh", "ctx"), P("ctx", "kvh")),
        check_vma=False,
    )
```

```python
import functools
import math

import jax
import jax.numpy as jnp
from jax import lax
from jax.experimental import pallas as pl
from jax.experimental.pallas import tpu as pltpu
from jax.sharding import PartitionSpec as P

MESH = pl.DeviceIdType.MESH
HD = 128
TOK = 512
BF = jnp.bfloat16
F32 = jnp.float32
KV, GATE, UP, DOWN = range(4)
LOG2E = math.log2(math.e)
SCALE2 = LOG2E / math.sqrt(HD)

ORDER = (
    "st", "K0", "K12", "U0", "U12", "G0", "Fs", "F0a", "K4", "G2", "K1", "F1a", "U1", "U13", "U2",
    "F2a", "G1", "U14", "U4", "K2", "F0b", "Qs", "U5", "G3", "K8", "Kr0", "U8", "U3", "U6", "D0",
    "Ur0", "F1b", "F2b", "Q", "G4", "U15", "A00", "G5", "G6", "U9", "A01", "A02", "F3", "G8", "K3",
    "N", "A03", "Gr1", "U7", "U10", "D2", "K13", "Gr0", "PG0", "PG1", "PU0", "Ur2", "K5", "D1",
    "G7", "K15", "PU2", "Gr2", "K14", "U11", "Ur1", "PG2", "PU1", "Gr3", "PG3", "D3", "Ur3", "PU3",
    "ACT", "Dr0", "W02", "W00", "D4", "W03", "K9", "K6", "W01", "D6", "D5", "K7", "D8", "X01",
    "X00", "Kr1", "A10", "A11", "Dr1", "W12", "W10", "A12", "K10", "Dr2", "W11", "W22", "A13",
    "X10", "W20", "Kr2", "D7", "K11", "A20", "X11", "A21", "W13", "Dr3", "W21", "X21", "X20", "W23",
    "Kr3", "W32", "C0", "C1", "W31", "A22", "A23", "A30", "W30", "C2", "A31", "X30", "X31", "A32",
    "A33", "AF", "E0", "W33", "C3", "E1", "E2", "E3",
)


def kernel(
    span_ref, gain_ref, q_in, k_in, v_in, f_in, g_in, u_in, d_in,
    att_out, log_out, ffn_out,
    kv_b, g_b, u_b, d_b,
    q_b, f_b, n_b, m_b, acc_b, o_b, orx_b, lg_b, lrx_b,
    ga_b, ua_b, hid_b, ps_b, po_b, fr_b, rs_b, r_b, rx_b, fo_b,
    loc_sem, send_sem, recv_sem, xs_sem, xr_sem,
):
    ctx = lax.axis_index("ctx")
    kvh = lax.axis_index("kvh")
    x, c = kvh // 2, kvh % 2
    y, z = ctx // 4, ctx % 4
    h = y // 2
    same = c * h + (1 - c) * (1 - h)
    is_same = c == h
    not_same = c != h
    yp = y + 1 - 2 * (y % 2)
    yo = 3 - y
    yq = (y + 2) % 4
    yt = same * y + (1 - same) * yo

    def dev(xx, yy, zz, cc):
        return {"ctx": yy * 4 + zz, "kvh": xx * 2 + cc}

    zr, zl, zf = (z + 1) % 4, (z + 3) % 4, (z + 2) % 4
    xr, xl = (x + 1) % 4, (x + 3) % 4
    SIB = dev(x, y, z, 1 - c)
    PART = dev(x, yp, z, c)
    OPP = dev(x, yo, z, c)
    OPPD = dev(x, yo, z, 1 - c)
    ZR, ZL = dev(x, y, zr, c), dev(x, y, zl, c)
    XR, XL = dev(xr, y, z, c), dev(xl, y, z, c)

    barrier = pltpu.get_barrier_semaphore()
    for t in (SIB, PART, OPP, OPPD, ZR, ZL, XR, XL):
        pl.semaphore_signal(barrier, inc=1, device_id=t, device_id_type=MESH)
    pl.semaphore_wait(barrier, 8)

    def remote(src, dst, ss, rs, target):
        return pltpu.make_async_remote_copy(
            src_ref=src, dst_ref=dst, send_sem=ss, recv_sem=rs,
            device_id=target, device_id_type=MESH,
        )

    bufs = (kv_b, g_b, u_b, d_b)
    ins = (None, g_in, u_in, d_in)
    groups = (z, zl, zr, zf)
    own = 4 * z + y
    extra = (16 + z, 16, 16 + z, 16)
    yb = (y, yp, yo, yq)
    P0 = 2 * h
    P1 = 2 - 2 * h
    sent = {}

    def copy_of(a, idx, half=0):
        def cp(s, d, target, count=1):
            if count == 1:
                src, dst = bufs[a].at[s, c], bufs[a].at[d, c]
            else:
                src = bufs[a].at[pl.ds(s, count), c]
                dst = bufs[a].at[pl.ds(d, count), c]
            return remote(src, dst, send_sem.at[a, idx], recv_sem.at[a, idx], target)

        if idx == 0:
            slot = same * own + (1 - same) * extra[a]
            src = (v_in, k_in)[half] if a == KV else ins[a].at[1 - c]
            return remote(
                src, bufs[a].at[slot, 1 - c], send_sem.at[a, 0], recv_sem.at[a, 0], SIB
            )
        if idx in (17, 18) and a not in (KV, UP):
            s = 4 * zf + (P0 if idx == 17 else P1)
            return cp(s, s, SIB, 2)
        if 14 <= idx < 18:
            s = 4 * groups[idx - 14]
            return cp(s, s, SIB, 4)
        if a in (KV, UP):
            if idx in (4, 6):
                return cp(own, own, ZR if idx == 4 else ZL)
            if idx in (5, 7):
                return cp(16 + z, 16 + z, ZR if idx == 5 else ZL)
            if idx == 8:
                return cp(4 * zl + y, 4 * zl + y, ZR)
            if idx == 9:
                return cp(16 + zr, 16 + zr, ZL)
            zs = groups[idx % 4]
            if 20 <= idx < 24:
                return cp(4 * zs + y, 4 * zs + y, PART)
            if 24 <= idx < 28:
                return cp(16 + zs, 4 * zs + y, OPP)
            return cp(4 * zs + yo, 4 * zs + yo, PART)
        if idx == 1:
            return cp(own, own, PART)
        if idx == 2:
            return cp(16, own, OPP)
        if idx == 3:
            return cp(4 * z + yo, 4 * z + yo, PART)
        if 4 <= idx < 12:
            s = 4 * z + yb[idx % 4]
            return cp(s, s, ZR if idx < 8 else ZL)
        if idx == 12:
            return cp(4 * zl + P0, 4 * zl + P0, ZR, 2)
        return cp(4 * zr + P1, 4 * zr + P1, ZL, 2)

    def local_of(a, half=0):
        slot = same * own + (1 - same) * extra[a]
        src = (k_in, v_in)[half] if a == KV else ins[a].at[c]
        return pltpu.make_async_copy(src, bufs[a].at[slot, c], loc_sem.at[a])

    def go(a, *idxs):
        for idx in idxs:
            copy_of(a, idx).start()
            sent[a, idx] = True

    def got(a, *idxs):
        for idx in idxs:
            copy_of(a, idx).wait_recv()

    def first(a, mine, other):
        local_of(a).wait()
        pl.when(is_same)(lambda: go(a, *mine))
        pl.when(not_same)(lambda: go(a, *other))
        got(a, 0)
        pl.when(is_same)(lambda: go(a, *other))
        pl.when(not_same)(lambda: go(a, *mine))

    def ev_z(a, n):
        if n == 0:
            first(a, (1, 4, 8), (2,))
        elif n == 1:
            got(a, 1)
            go(a, 5, 9)
        elif n == 2:
            got(a, 2)
            go(a, 3, 6, 10)
        elif n == 3:
            got(a, 3)
            go(a, 7, 11, 14)
        elif n == 4:
            got(a, 4, 5)
            go(a, 12)
        elif n == 5:
            got(a, 10, 11)
            go(a, 13)
        elif n == 6:
            got(a, 6, 7)
            go(a, 15)
        elif n == 8:
            got(a, 8, 9)
            go(a, 16)
        elif n == 7:
            got(a, 12)
            go(a, 17)
            got(a, 13)
            go(a, 18)

    def ev_y(a, n):
        if n == 0:
            first(a, (4, 6), (5, 7))
        elif n == 1:
            got(a, 4, 5)
            go(a, 8)
        elif n == 2:
            got(a, 6, 7)
            go(a, 9)
        elif n == 3:
            got(a, 8, 9)
        elif n < 8:
            got(a, 20 + n)
            go(a, 24 + n)
        elif n >= 12:
            go(a, 8 + n, 12 + n)
        else:
            got(a, 12 + n, 20 + n)
            go(a, 6 + n)

    k0 = 2 * x + c
    two = pl.ds(2 * x, 2)
    left, right = pl.ds(0, 128), pl.ds(128, 128)

    def out_copy(g):
        return remote(o_b.at[g], orx_b.at[g], xs_sem.at[42 + g], xr_sem.at[42 + g], OPPD)

    def xc(i):
        def cp(src, dst, target):
            return remote(src, dst, xs_sem.at[i], xr_sem.at[i], target)

        if i == 0:
            return cp(f_in, f_b.at[k0], SIB)
        if i in (1, 2):
            return remote(
                f_in, f_b.at[k0], xs_sem.at[1], xr_sem.at[1 + c], OPP if i == 1 else OPPD
            )
        if i == 3:
            return cp(q_in, q_b, OPPD)
        if i in (4, 5):
            return cp(f_b.at[two], f_b.at[two], XR if i == 4 else XL)
        if i == 6:
            return cp(f_b.at[2 * xl], f_b.at[2 * xl], XR)
        if i == 7:
            return cp(f_b.at[2 * xr + 1], f_b.at[2 * xr + 1], XL)
        if i == 9:
            return cp(lg_b, lrx_b, OPPD)
        if i < 14 or i >= 54:
            n, cols = (i - 10, left) if i < 14 else (i - 54, right)
            core = {"ctx": yo * 4 + z, "kvh": 2 * x + groups[n] // 2}
            return cp(r_b.at[n, :, cols], rx_b.at[n, :, cols], core)
        if i < 18:
            return cp(r_b.at[i - 14], fo_b.at[i - 14], SIB)
        g, n = (i - 18) // 6, (i - 18) % 6
        lo, hi = pl.ds(0, 256), pl.ds(256, 256)
        if i >= 46:
            g, n = (i - 46) // 2, (i - 46) % 2
            rows = hi if n else lo
            return cp(ps_b.at[g, n, rows, right], rs_b.at[g, n, rows, right], XL if n else XR)
        if n == 0:
            return cp(ps_b.at[g, 2, lo], fr_b.at[g, 0], XR)
        if n == 1:
            return cp(ps_b.at[g, 2, hi], fr_b.at[g, 1], XL)
        if n == 2:
            return cp(ps_b.at[g, 0, hi], rs_b.at[g, 0, hi], XR)
        if n == 3:
            return cp(ps_b.at[g, 1, lo], rs_b.at[g, 1, lo], XL)
        if n == 4:
            return cp(ps_b.at[g, 0, lo, left], rs_b.at[g, 0, lo, left], XR)
        return cp(ps_b.at[g, 1, hi, left], rs_b.at[g, 1, hi, left], XL)

    f_loc = pltpu.make_async_copy(f_in, f_b.at[k0], loc_sem.at[4])
    q_loc = pltpu.make_async_copy(q_in, q_b, loc_sem.at[5])

    def start():
        @pl.when(is_same)
        def _():
            f_loc.start()

        @pl.when(not_same)
        def _():
            xc(0).start()

        for half in range(2):
            @pl.when(c == half)
            def _():
                local_of(KV, half).start()
                copy_of(KV, 0, half).start()

        sent[KV, 0] = True
        for a in (GATE, UP, DOWN):
            local_of(a).start()
            go(a, 0)

    def feat(nm):
        if nm == "Fs":
            pl.when(is_same)(lambda: xc(1).start())
            pl.when(not_same)(lambda: xc(2).start())
            return
        n = nm[1]
        if n == "3":
            xc(6).wait_recv()
            xc(7).wait_recv()
            return

        @pl.when(is_same if nm[2] == "a" else not_same)
        def _():
            if nm == "F0a":
                f_loc.wait()
                xc(0).wait_recv()
            elif nm == "F0b":
                for j in range(2):
                    remote(f_in, f_b.at[0], xs_sem.at[1], xr_sem.at[1 + j], OPP).wait_recv()
            if n == "0":
                xc(4).start()
                xc(5).start()
            elif n == "1":
                xc(4).wait_recv()
                xc(6).start()
            else:
                xc(5).wait_recv()
                xc(7).start()

    def q_wait():
        pl.when(is_same)(lambda: q_loc.wait())
        pl.when(not_same)(lambda: xc(3).wait())

    my_span = span_ref[yt * 4 + z]

    step = 128

    def tile(g, t, q, k, va, hide, first):
        rows = slice(t * step, t * step + step)
        s = lax.dot_general(q, k, (((1,), (1,)), ((), ())), preferred_element_type=F32)
        if first:
            ri = lax.broadcasted_iota(jnp.int32, (step, TOK), 0) + t * step
            ci = lax.broadcasted_iota(jnp.int32, (step, TOK), 1)
            s = jnp.where(ci <= ri, s, -1e30)
            m_new = jnp.broadcast_to(jnp.max(s, axis=1, keepdims=True), (step, HD)) * SCALE2
            p = jnp.exp2(s * SCALE2 - jnp.concatenate([m_new] * 4, axis=1))
            acc_b[g, rows] = jnp.dot(p.astype(BF), va, preferred_element_type=F32)
        else:
            m_old = m_b[g, rows]
            top = jnp.max(s, axis=1, keepdims=True) * SCALE2 - hide
            m_new = jnp.maximum(m_old, top)
            alpha = jnp.exp2(m_old - m_new)
            sub = m_new + hide
            p = jnp.exp2(s * SCALE2 - jnp.concatenate([sub] * 4, axis=1))
            pv = jnp.dot(p.astype(BF), va, preferred_element_type=F32)
            acc_b[g, rows] = acc_b[g, rows] * jnp.concatenate([alpha] * 2, axis=1) + pv
        m_b[g, rows] = m_new

    def operands(slot, src):
        hide = jnp.where(span_ref[src] < my_span, 0.0, 1e30).astype(F32)
        k = kv_b[slot, 0]
        return hide, k, jnp.concatenate([kv_b[slot, 1], jnp.ones((TOK, HD), BF)], axis=1)

    def attend(slot, src, first):
        hide, k, va = operands(slot, src)
        for g in range(4):
            for t in range(TOK // step):
                q = q_b[t * step : t * step + step, g * HD : g * HD + HD]
                tile(g, t, q, k, va, hide, first)

    def attend_head(g):
        col = pl.ds(pl.multiple_of(g * HD, HD), HD)
        for ys in range(4):
            hide, k, va = operands(4 * zf + ys, 4 * ys + zf)
            for t in range(TOK // step):
                tile(g, t, q_b[t * step : t * step + step, col], k, va, hide, False)
        total = acc_b[g, :, HD:]
        o_b[g] = (acc_b[g, :, :HD] / total).astype(BF)
        logs = m_b[g] * (1.0 / LOG2E) + jnp.log(total)
        lg_b[g] = jnp.transpose(logs)[:8]

        @pl.when(not_same)
        def _():
            out_copy(g).start()

    def finish():
        @pl.when(is_same)
        def _():
            for g in range(4):
                att_out[:, g * HD : g * HD + HD] = o_b[g]
                log_out[pl.ds(g, 1)] = lg_b[g, :1]

        @pl.when(not_same)
        def _():
            xc(9).start()

    def norm():
        gains = [gain_ref[k * TOK : (k + 1) * TOK].reshape(1, TOK) for k in range(8)]

        def rows_of(i, _):
            rows = pl.ds(i * 64, 64)
            part = jnp.zeros((64, TOK), F32)
            for k in range(8):
                v = f_b[k, rows].astype(F32)
                part = part + v * v
            r = lax.rsqrt(jnp.sum(part, axis=1, keepdims=True) * (1.0 / 4096) + 1e-05)
            for k in range(8):
                n_b[k, rows] = (f_b[k, rows].astype(F32) * r * gains[k]).astype(BF)
            return 0

        lax.fori_loop(0, 8, rows_of, 0)

    def project(a, i):
        zs = groups[i]
        out = ga_b if a == GATE else ua_b
        off = pl.multiple_of((zs % 2) * 256, 256)

        def rows_of(t, _):
            rows = pl.ds(t * 256, 256)
            lhs = jnp.concatenate(
                [n_b[2 * ys + zs // 2, rows, pl.ds(off, 256)] for ys in range(4)], axis=1
            )
            w = bufs[a][pl.ds(4 * zs, 4)].reshape(1024, 896)
            res = jnp.dot(lhs, w, preferred_element_type=F32)
            if i == 0:
                out[rows] = res
            else:
                out[rows] = out[rows] + res
            return 0

        lax.fori_loop(0, 2, rows_of, 0)

    def act():
        def rows_of(i, _):
            rows = pl.ds(i * 64, 64)
            g = ga_b[rows]
            hid_b[rows] = (g / (1.0 + jnp.exp(-g)) * ua_b[rows]).astype(BF)
            return 0

        lax.fori_loop(0, 8, rows_of, 0)

    def x_go(i, *ns):
        for n in ns:
            xc(18 + 6 * i + n).start()
            sent[18 + 6 * i + n] = True

    def x_got(i, *ns):
        for n in ns:
            xc(18 + 6 * i + n).wait_recv()

    def down(i, n):
        xd = (xr, xl, (x + 2) % 4, x)[n]
        w = d_b[4 * groups[i] + xd].reshape(896, 256)
        res = jnp.dot(hid_b[...], w, preferred_element_type=F32)
        if n == 3:
            po_b[i] = res
            return
        ps_b[i, n] = res.astype(BF)
        if n == 2:
            x_go(i, 0, 1)
        else:
            x_go(i, 2 + n)

    def forward(i, n):
        x_got(i, n)
        rows = pl.ds(256 * n, 256)
        ps_b[i, n, rows] = (ps_b[i, n, rows].astype(F32) + fr_b[i, n].astype(F32)).astype(BF)
        x_go(i, 4 + n)
        xc(46 + 2 * i + n).start()
        sent[46 + 2 * i + n] = True

    def combine(i):
        x_got(i, 2, 3)
        for m, cols in enumerate((left, right)):
            if m == 0:
                x_got(i, 4, 5)
            else:
                xc(46 + 2 * i).wait_recv()
                xc(47 + 2 * i).wait_recv()
            total = po_b[i, :, cols] + rs_b[i, 0, :, cols].astype(F32)
            r_b[i, :, cols] = (total + rs_b[i, 1, :, cols].astype(F32)).astype(BF)

            @pl.when(not_same)
            def _():
                xc(10 + i + 44 * m).start()

        @pl.when(is_same & (groups[i] // 2 != c))
        def _():
            xc(14 + i).start()

    def close(i):
        zs = groups[i]

        @pl.when(zs // 2 == c)
        def _():
            pl.when(not_same)(lambda: xc(14 + i).wait_recv())
            for m, cols in enumerate((left, right)):
                xc(10 + i + 44 * m).wait_recv()
                out = pl.ds(pl.multiple_of((zs % 2) * 256 + 128 * m, 128), 128)

                @pl.when(is_same)
                def _():
                    res = r_b[i, :, cols].astype(F32) + rx_b[i, :, cols].astype(F32)
                    ffn_out[:, out] = res.astype(BF)

                @pl.when(not_same)
                def _():
                    res = fo_b[i, :, cols].astype(F32) + rx_b[i, :, cols].astype(F32)
                    ffn_out[:, out] = res.astype(BF)

    def run(nm):
        if nm == "st":
            start()
        elif nm[0] == "F":
            feat(nm)
        elif nm == "Qs":
            pl.when(is_same)(lambda: q_loc.start())
            pl.when(not_same)(lambda: xc(3).start())
        elif nm == "Q":
            q_wait()
        elif nm == "AF":
            finish()
        elif nm == "N":
            norm()
        elif nm == "ACT":
            act()
        elif nm[0] == "P":
            project("KGUD".index(nm[1]), int(nm[2]))
        elif nm[0] == "W":
            down(int(nm[1]), int(nm[2]))
        elif nm[0] == "X":
            forward(int(nm[1]), int(nm[2]))
        elif nm[0] == "C":
            combine(int(nm[1]))
        elif nm[0] == "E":
            close(int(nm[1]))
        else:
            a = "KGUD".index(nm[0])
            if nm[1] == "r":
                got(a, 14 + int(nm[2]))
                if nm[2] == "3" and a not in (KV, UP):
                    got(a, 18)
            elif a in (KV, UP):
                ev_y(a, int(nm[1:]))
            else:
                ev_z(a, int(nm[1:]))

    parts = [[]]
    for nm in ORDER:
        if nm[0] == "A" and nm[1:].isdigit():
            parts.append([])
        else:
            parts[-1].append(nm)
    for nm in parts[0]:
        run(nm)
    attend(4 * z + yt, yt * 4 + z, True)
    for nm in parts[1]:
        run(nm)

    def block(n, _):
        i, j = n // 4, n % 4
        delta = (i // 2) * (i - 1) + (1 - i // 2) * (3 * i)
        zs = (z + delta) % 4
        ys = (yt + j) % 4
        attend(4 * zs + ys, ys * 4 + zs, False)
        for m in range(1, 12):
            if parts[m + 1]:
                @pl.when(n == m)
                def _():
                    for nm in parts[m + 1]:
                        run(nm)
        return 0

    lax.fori_loop(1, 12, block, 0)

    def last(g, _):
        attend_head(g)
        for m in range(3):
            if parts[13 + m]:
                @pl.when(g == m)
                def _():
                    for nm in parts[13 + m]:
                        run(nm)
        return 0

    lax.fori_loop(0, 4, last, 0)
    for nm in parts[16]:
        run(nm)

    @pl.when(is_same)
    def _():
        xc(1).wait_send()
        for i in range(4):
            pl.when(groups[i] // 2 != c)(lambda: xc(14 + i).wait_send())

    @pl.when(not_same)
    def _():
        xc(0).wait_send()
        xc(2).wait_send()
        xc(9).wait()
        for g in range(4):
            log_out[pl.ds(g, 1)] = lrx_b[g, :1]
            out_copy(g).wait()
            att_out[:, g * HD : g * HD + HD] = orx_b[g]
        for i in range(4):
            xc(10 + i).wait_send()
            xc(54 + i).wait_send()

    for i in (4, 5, 6, 7):
        xc(i).wait_send()
    for it in sent:
        if isinstance(it, tuple):
            copy_of(*it).wait_send()
        else:
            xc(it).wait_send()


def move(a_in, l_in, f_in, a_out, l_out, f_out):
    a_out[...] = a_in[...]
    l_out[...] = l_in[...]
    f_out[...] = f_in[...]


def body(queries, keys, values, span_order, ffn_input, norm_gain, gate_w, up_w, down_w):
    anyspace = pl.BlockSpec(memory_space=pl.ANY)
    vmem = pl.BlockSpec(memory_space=pltpu.VMEM)
    smem = pl.BlockSpec(memory_space=pltpu.SMEM)
    sem = pltpu.SemaphoreType.DMA
    shapes = (
        jax.ShapeDtypeStruct((512, 512), BF),
        jax.ShapeDtypeStruct((4, 512), F32),
        jax.ShapeDtypeStruct((512, 512), BF),
    )
    outs = pl.pallas_call(
        kernel,
        out_shape=shapes,
        in_specs=[smem, vmem] + [anyspace] * 7,
        out_specs=(vmem, vmem, vmem),
        scratch_shapes=[
            pltpu.VMEM((20, 2, 512, 128), BF),
            pltpu.VMEM((17, 2, 128, 896), BF),
            pltpu.VMEM((20, 2, 128, 896), BF),
            pltpu.VMEM((17, 2, 448, 256), BF),
            pltpu.VMEM((512, 512), BF),
            pltpu.VMEM((8, 512, 512), BF),
            pltpu.VMEM((8, 512, 512), BF),
            pltpu.VMEM((4, 512, 128), F32),
            pltpu.VMEM((4, 512, 256), F32),
            pltpu.VMEM((4, 512, 128), BF),
            pltpu.VMEM((4, 512, 128), BF),
            pltpu.VMEM((4, 8, 512), F32),
            pltpu.VMEM((4, 8, 512), F32),
            pltpu.VMEM((512, 896), F32),
            pltpu.VMEM((512, 896), F32),
            pltpu.VMEM((512, 896), BF),
            pltpu.VMEM((4, 3, 512, 256), BF),
            pltpu.VMEM((4, 512, 256), F32),
            pltpu.VMEM((4, 2, 256, 256), BF),
            pltpu.VMEM((4, 2, 512, 256), BF),
            pltpu.VMEM((4, 512, 256), BF),
            pltpu.VMEM((4, 512, 256), BF),
            pltpu.VMEM((4, 512, 256), BF),
            sem((6,)),
            sem((4, 32)),
            sem((4, 32)),
            sem((58,)),
            sem((58,)),
        ],
        compiler_params=pltpu.CompilerParams(
            collective_id=0, has_side_effects=True, vmem_limit_bytes=63 * 2**20
        ),
        name="layer",
    )(
        span_order,
        norm_gain,
        queries,
        keys,
        values,
        ffn_input,
        gate_w.reshape(2, 128, 896),
        up_w.reshape(2, 128, 896),
        down_w.reshape(2, 448, 256),
    )
    return pl.pallas_call(
        move,
        out_shape=shapes,
        in_specs=[vmem] * 3,
        out_specs=(vmem,) * 3,
        name="move",
    )(*outs)


def solution(mesh):
    placed = (
        P("ctx", "kvh"), P("ctx", "kvh"), P("ctx", "kvh"), P(), P("ctx", "kvh"), P(),
        P("ctx", "kvh"), P("ctx", "kvh"), P("kvh", "ctx"),
    )
    return jax.shard_map(
        body,
        mesh=mesh,
        in_specs=placed,
        out_specs=(P("ctx", "kvh"), P("kvh", "ctx"), P("ctx", "kvh")),
        check_vma=False,
    )
```
